32 devices in a mesh: leaf: 8 (over z, y), front: 4 (over x, core).
Axes of the slice: x: 2, y: 2, z: 4, core: 2. Of those that a mesh axis runs over, the one named last changes fastest.
Arguments:
- rhs_sub: float32 [8, 65536], P(None, ('leaf', 'front')), may hold values from -6 to 6
- rhs_sep: float32 [8, 16384], P(None, 'leaf'), may hold values from -6 to 6
- live_rows: int32 [32], P(('leaf', 'front')), may hold values from 256 to 2048, as said below
- lower_inv: bfloat16 [256, 256, 256], P(('leaf', 'front')), as said below
- upper_inv: bfloat16 [256, 256, 256], P(('leaf', 'front'))
- couple_low: bfloat16 [2048, 16384], P(('leaf', 'front')), may hold values from -0.25 to 0.25
- couple_up: bfloat16 [2048, 16384], P(('leaf', 'front')), may hold values from -0.046875 to 0.046875
- sep_lower_inv: bfloat16 [16384, 16384], P('leaf', 'front')
- sep_upper_inv: bfloat16 [16384, 16384], P('leaf', 'front')
- basis_sub: float32 [48, 65536], P(None, ('leaf', 'front')), may hold values from -0.01953125 to 0.01953125
- basis_sep: float32 [48, 16384], P(None, 'leaf'), may hold values from -0.01953125 to 0.01953125
Outputs:
- orth_sub: float32 [8, 65536], P(None, ('leaf', 'front'))
- orth_sep: float32 [8, 16384], P(None, 'leaf')
- coef: float32 [48, 8], replicated
The draws below stay inside these ranges and needn't reach their ends.
Inputs may be any that keep to these rules, and one draw needn't show every extreme that they name: `live_rows`: each entry is a multiple of 256; some device has all 2048 rows live. Every block of lower_inv is lower triangular, and every block of upper_inv, sep_lower_inv and sep_upper_inv upper triangular, each with a diagonal between 1 and 1.5.
All inputs are finite; a program needn't handle non-finite values.
Results may differ from the reference program's by a relative error of at most 0.0055.
Values may be sent and summed in bfloat16 or wider, within the bound.
A program may use at most 128 MiB of HBM per device.

```python
import math
import jax
import jax.numpy as jnp
from jax import lax

VECS = 8
BASIS = 48
FRONT_ROWS = 256
BORDER = 64
SEP = 16384
ROWS_DEV = 2048
FRONTS = 8
TOTAL_ROWS = 65536
DEVICES = 32


def triangle(seed_key, block_count, size_order, upper_side):
    positions = jnp.arange(size_order)
    if upper_side:
        kept_part = positions[None, :] >= positions[:, None]
    else:
        kept_part = positions[None, :] <= positions[:, None]
    values = jax.random.normal(seed_key, (block_count, size_order, size_order), jnp.float32)
    values = values * (1.0 / math.sqrt(size_order))
    diagonal = 1.0 + 0.5 * jax.random.uniform(jax.random.fold_in(seed_key, 3), (block_count, size_order, 1), jnp.float32)
    on_diagonal = positions[None, :] == positions[:, None]
    return jnp.where(on_diagonal, diagonal, jnp.where(kept_part, values, 0.0))


def draw_live_rows(key, part):
    tiles = jax.random.randint(key, (DEVICES,), 1, FRONTS + 1) * FRONT_ROWS
    chosen = jax.random.randint(jax.random.fold_in(key, 7), (), 0, DEVICES)
    return jnp.where(jnp.arange(DEVICES) == chosen, ROWS_DEV, tiles).astype(jnp.int32)


def draw_lower_inv(key, part):
    return triangle(jax.random.fold_in(key, 11), DEVICES * FRONTS, FRONT_ROWS, False).astype(jnp.bfloat16)


def draw_upper_inv(key, part):
    return triangle(jax.random.fold_in(key, 12), DEVICES * FRONTS, FRONT_ROWS, True).astype(jnp.bfloat16)


def draw_sep_lower_inv(key, part):
    return triangle(jax.random.fold_in(key, 13), 1, SEP, True).reshape(SEP, SEP).astype(jnp.bfloat16)


def draw_sep_upper_inv(key, part):
    return triangle(jax.random.fold_in(key, 14), 1, SEP, True).reshape(SEP, SEP).astype(jnp.bfloat16)


def raised(result, stream_key, source, target, blocks, factor):
    def block_of(position):
        return (jnp.arange(result.shape[position]) // (result.shape[position] // blocks)).reshape((-1,) + (1,) * (result.ndim - 1 - position))

    first = jax.random.permutation(stream_key, blocks)[block_of(target)]
    second = (block_of(target) + blocks // 2) % blocks
    return jnp.where((block_of(source) == first) | (block_of(source) == second), factor * result, result)


def block_scale(stream_key, shape, pieces, smallest, largest):
    level, own = 1.0, jax.random.fold_in(stream_key, 6)
    for position, parts in pieces:
        draws = jnp.exp(jax.random.uniform(jax.random.fold_in(own, position), (parts,), jnp.float32, smallest / len(pieces), largest / len(pieces)))
        level = level * jnp.repeat(draws, shape[position] // parts).reshape([-1 if axis == position else 1 for axis in range(len(shape))])
    return level


def centred(own_key, dims, width, reach, pieces=(), held_as=jnp.bfloat16):
    level = block_scale(own_key, dims, pieces, -0.22, 0.18) if pieces else 1.0
    array = jax.random.normal(own_key, dims, jnp.float32) * width * level
    return jnp.minimum(jnp.maximum(array, -reach), reach).astype(held_as)


def bell_draw_with(own_key, shape, spread, most, shards, heavy, kind=jnp.bfloat16):
    entries = spread * jax.random.normal(own_key, shape, jnp.float32)
    if shards:
        entries = entries * block_scale(own_key, shape, shards, -0.22, 0.18)
    return jnp.clip(raised(entries, jax.random.fold_in(own_key, 3), *heavy), -most, most).astype(kind)


def setup_inputs(seed: int = 0) -> dict:
    splits = jax.random.split(jax.random.key(seed), 12)
    return {
        "rhs_sub": centred(splits[0], (VECS, TOTAL_ROWS), 1.0, 6.0, ((1, 32),), jnp.float32),
        "rhs_sep": centred(splits[1], (VECS, SEP), 1.0, 6.0, ((1, 8),), jnp.float32),
        "live_rows": draw_live_rows(jax.random.fold_in(splits[11], 71), 0),
        "lower_inv": draw_lower_inv(jax.random.fold_in(splits[11], 71), 0),
        "upper_inv": draw_upper_inv(jax.random.fold_in(splits[11], 71), 0),
        "couple_low": bell_draw_with(splits[5], (DEVICES * BORDER, SEP), (DEVICES * BORDER) ** -0.5, 0.25, ((0, 32),), (0, 1, 32, 2.75)),
        "couple_up": centred(splits[6], (DEVICES * BORDER, SEP), SEP ** -0.5, 0.046875, ((0, 32),)),
        "sep_lower_inv": draw_sep_lower_inv(jax.random.fold_in(splits[11], 71), 0),
        "sep_upper_inv": draw_sep_upper_inv(jax.random.fold_in(splits[11], 71), 0),
        "basis_sub": centred(splits[9], (BASIS, TOTAL_ROWS), (TOTAL_ROWS + SEP) ** -0.5, 0.01953125, ((1, 32),), jnp.float32),
        "basis_sep": centred(splits[10], (BASIS, SEP), (TOTAL_ROWS + SEP) ** -0.5, 0.01953125, ((1, 8),), jnp.float32),
    }


def apply_blocks(vectors, inverse):
    vec_count = vectors.shape[0]
    shaped = vectors.astype(jnp.bfloat16).astype(jnp.float32).reshape(vec_count, inverse.shape[0], inverse.shape[1])
    product = jnp.einsum("vkr,krc->vkc", shaped, inverse.astype(jnp.float32))
    return product.reshape(vec_count, inverse.shape[0] * inverse.shape[2])


def reference(rhs_sub, rhs_sep, live_rows, lower_inv, upper_inv, couple_low, couple_up, sep_lower_inv, sep_upper_inv, basis_sub, basis_sep):
    vec_count = rhs_sub.shape[0]
    row_number = jnp.arange(ROWS_DEV, dtype=jnp.int32)
    live_mask = (row_number[None, :] < live_rows[:, None]).reshape(1, DEVICES * ROWS_DEV)
    lower_sol = jnp.where(live_mask, apply_blocks(rhs_sub, lower_inv), 0.0)
    per_device = lower_sol.reshape(vec_count, DEVICES, ROWS_DEV)
    border_rows = per_device[:, :, :BORDER].reshape(vec_count, DEVICES * BORDER).astype(jnp.bfloat16)
    top_rhs = rhs_sep - jnp.dot(border_rows, couple_low, preferred_element_type=jnp.float32)
    top_lower = jnp.dot(top_rhs.astype(jnp.bfloat16), sep_lower_inv, preferred_element_type=jnp.float32)
    top_sol = lax.dot_general(top_lower.astype(jnp.bfloat16), sep_upper_inv, (((1,), (1,)), ((), ())), preferred_element_type=jnp.float32)
    correction = lax.dot_general(top_sol.astype(jnp.bfloat16), couple_up, (((1,), (1,)), ((), ())), preferred_element_type=jnp.float32)
    correction = correction.reshape(vec_count, DEVICES, BORDER)
    updated = jnp.concatenate([per_device[:, :, :BORDER] - correction, per_device[:, :, BORDER:]], axis=2)
    updated = updated.reshape(vec_count, DEVICES * ROWS_DEV)
    upper_sol = jnp.where(live_mask, apply_blocks(updated, upper_inv), 0.0)
    coef_sum = jnp.zeros((BASIS, vec_count), jnp.float32)
    high = lax.Precision.HIGHEST
    for sweep in range(2):
        coef_pass = jnp.dot(basis_sub, upper_sol.T, precision=high) + jnp.dot(basis_sep, top_sol.T, precision=high)
        upper_sol = upper_sol - jnp.dot(coef_pass.T, basis_sub, precision=high)
        top_sol = top_sol - jnp.dot(coef_pass.T, basis_sep, precision=high)
        coef_sum = coef_sum + coef_pass
    return (upper_sol, top_sol, coef_sum)
```

```python
import functools

import jax
import jax.numpy as jnp
from jax import lax
from jax.experimental import pallas as pl
from jax.experimental.pallas import tpu as pltpu
from jax.sharding import PartitionSpec as P

MESH = pl.DeviceIdType.MESH
HIGH = lax.Precision.HIGHEST
LAST = (((1,), (1,)), ((), ()))
A_SUM, A_ALL, B_SUM, B_ALL, C_SUM, S_ALL, D_ALL, G_FRONT, G_LEAF, H_ALL = range(10)


def fold(piece):
    half = piece.shape[1] // 2
    return jnp.concatenate([piece[:, :half], piece[:, half:]], axis=0)


def unfold(piece):
    piece = piece.astype(jnp.float32)
    rows = piece.shape[0] // 2
    return jnp.concatenate([piece[:rows], piece[rows:]], axis=1)


def exact(left, right, dims=LAST):
    return lax.dot_general(left, right, dims, precision=HIGH, preferred_element_type=jnp.float32)


def fused(
    leaves,
    fronts,
    live,
    rhs_sub,
    rhs_sep,
    lower_inv,
    upper_inv,
    couple_low,
    couple_up,
    sep_lower,
    sep_upper,
    basis_sub,
    basis_sep,
    orth_sub,
    orth_sep,
    coef,
    rhs_sub_v,
    rhs_sep_v,
    lower_v,
    upper_v,
    clow_v,
    cup_v,
    slow_v,
    sup_v,
    bsub_v,
    bsep_v,
    low_v,
    sol_v,
    a_send,
    a_recv,
    t_buf,
    b_send,
    b_recv,
    l_buf,
    c_send,
    c_recv,
    s_buf,
    d_buf,
    g_front,
    g_leaf,
    h_buf,
    load,
    send,
    recv,
):
    leaf, front = lax.axis_index("leaf"), lax.axis_index("front")
    count = leaves * fronts
    me = leaf * fronts + front
    blocks, size, _ = lower_v.shape
    border = clow_v.shape[0]
    width = s_buf.shape[2]
    basis = bsub_v.shape[0]

    def fetch(source, target, slot):
        return pltpu.make_async_copy(source, target, load.at[slot])

    def push(source, target, step, device):
        pltpu.make_async_remote_copy(
            src_ref=source,
            dst_ref=target,
            send_sem=send.at[step],
            recv_sem=recv.at[step],
            device_id=device,
            device_id_type=MESH,
        ).start()

    def drain(view, sem):
        pltpu.make_async_copy(view, view, sem).wait()

    def device(k):
        other = lax.rem(me + k, count)
        return other // fronts, lax.rem(other, fronts)

    def columns(index):
        return pl.ds(pl.multiple_of(index * width, width), width)

    first = [
        fetch(rhs_sub, rhs_sub_v, 0),
        fetch(lower_inv.at[pl.ds(0, 1)], lower_v.at[pl.ds(0, 1)], 1),
        fetch(couple_low, clow_v, 2),
    ]
    second = [
        fetch(rhs_sep, rhs_sep_v, 3),
        fetch(lower_inv.at[pl.ds(1, blocks - 1)], lower_v.at[pl.ds(1, blocks - 1)], 4),
        fetch(upper_inv, upper_v, 5),
        fetch(basis_sub, bsub_v, 6),
        fetch(basis_sep, bsep_v, 7),
    ]
    third = [fetch(sep_lower, slow_v, 8), fetch(sep_upper, sup_v, 9), fetch(couple_up, cup_v, 10)]
    for copy in first:
        copy.start()

    barrier = pltpu.get_barrier_semaphore()

    def greet(k, carry):
        pl.semaphore_signal(barrier, inc=1, device_id=device(k), device_id_type=MESH)
        return carry

    lax.fori_loop(1, count, greet, 0)
    for copy in second:
        copy.start()

    def live_part(value, k):
        row = lax.broadcasted_iota(jnp.int32, value.shape, 1) + k * size
        return jnp.where(row < live[0], value, 0.0)

    def lower_block(k):
        part = rhs_sub_v[:, k * size : (k + 1) * size].astype(jnp.bfloat16)
        return live_part(jnp.dot(part, lower_v[k], preferred_element_type=jnp.float32), k)

    def upper_block(value, k):
        part = value.astype(jnp.bfloat16)
        return live_part(jnp.dot(part, upper_v[k], preferred_element_type=jnp.float32), k)

    first[0].wait()
    first[1].wait()
    low_v[...] = lower_block(0)
    border_rows = low_v[:, :border].astype(jnp.bfloat16)
    first[2].wait()
    for copy in third:
        copy.start()
    pl.semaphore_wait(barrier, count - 1)

    def couple(index):
        return jnp.dot(border_rows, clow_v[:, columns(index)], preferred_element_type=jnp.float32)

    def a_step(k, carry):
        a_send[k - 1] = fold(couple(lax.rem(me + k, count))).astype(jnp.bfloat16)
        push(a_send.at[k - 1], a_recv.at[k - 1], A_SUM, device(k))
        return carry

    lax.fori_loop(1, count, a_step, 0)

    second[3].wait()
    second[4].wait()
    own = bsep_v[:, columns(front)]
    gram = exact(bsub_v[...], bsub_v[...]) + exact(own, own)
    g_front[front] = jnp.zeros(g_front.shape[1:], jnp.float32)
    g_front[front, :, 0:basis] = gram
    for k in range(1, fronts):
        push(g_front.at[front], g_front.at[front], G_FRONT, (leaf, lax.rem(front + k, fronts)))
    second[1].wait()
    second[2].wait()
    for k in range(1, blocks):
        sol_v[:, k * size : (k + 1) * size] = upper_block(lower_block(k), k)
    early = exact(sol_v[:, size:], bsub_v[:, size:])
    second[0].wait()
    top = rhs_sep_v[:, columns(front)] - couple(me)

    drain(a_recv, recv.at[A_SUM])
    top = fold(top) - jnp.sum(a_recv[...].astype(jnp.float32), axis=0)
    t_buf[front] = top.astype(jnp.bfloat16)
    for k in range(1, fronts):
        push(t_buf.at[front], t_buf.at[front], A_ALL, (leaf, lax.rem(front + k, fronts)))

    drain(g_front.at[pl.ds(0, fronts - 1)], recv.at[G_FRONT])
    g_leaf[leaf] = jnp.sum(g_front[...], axis=0)
    for k in range(1, leaves):
        push(g_leaf.at[leaf], g_leaf.at[leaf], G_LEAF, (lax.rem(leaf + k, leaves), front))

    third[0].wait()
    drain(t_buf.at[pl.ds(0, fronts - 1)], recv.at[A_ALL])
    rows = jnp.concatenate([unfold(t_buf[k]) for k in range(fronts)], axis=1).astype(jnp.bfloat16)

    def lower_piece(index):
        return jnp.dot(rows, slow_v[:, columns(index)], preferred_element_type=jnp.float32)

    def b_step(k, carry):
        to = lax.rem(leaf + k, leaves)
        b_send[k - 1] = lower_piece(to)
        push(b_send.at[k - 1], b_recv.at[k - 1], B_SUM, (to, front))
        return carry

    lax.fori_loop(1, leaves, b_step, 0)
    piece = lower_piece(leaf)
    drain(b_recv, recv.at[B_SUM])
    piece = piece + jnp.sum(b_recv[...], axis=0)
    l_buf[leaf] = fold(piece).astype(jnp.bfloat16)
    for k in range(1, leaves):
        push(l_buf.at[leaf], l_buf.at[leaf], B_ALL, (lax.rem(leaf + k, leaves), front))
    third[1].wait()
    drain(l_buf.at[pl.ds(0, leaves - 1)], recv.at[B_ALL])
    rows2 = jnp.concatenate([unfold(l_buf[k]) for k in range(leaves)], axis=1).astype(jnp.bfloat16)

    def upper_piece(index):
        part = sup_v[pl.ds(pl.multiple_of(index * width, width), width), :]
        return lax.dot_general(rows2, part, LAST, preferred_element_type=jnp.float32)

    def c_step(k, carry):
        to = lax.rem(front + k, fronts)
        c_send[k - 1] = upper_piece(to)
        push(c_send.at[k - 1], c_recv.at[k - 1], C_SUM, (leaf, to))
        return carry

    lax.fori_loop(1, fronts, c_step, 0)
    piece = upper_piece(front)
    drain(c_recv, recv.at[C_SUM])
    piece = piece + jnp.sum(c_recv[...], axis=0)
    d_buf[me] = fold(piece).astype(jnp.bfloat16)

    def d_step(k, carry):
        push(d_buf.at[me], d_buf.at[me], D_ALL, device(k))
        return carry

    lax.fori_loop(1, count, d_step, 0)
    s_buf[front] = piece
    for k in range(1, fronts):
        push(s_buf.at[front], s_buf.at[front], S_ALL, (leaf, lax.rem(front + k, fronts)))
    early = early + exact(piece, bsep_v[:, columns(front)])
    third[2].wait()

    drain(d_buf.at[pl.ds(0, count - 1)], recv.at[D_ALL])

    def correct(k, total):
        part = unfold(d_buf[k]).astype(jnp.bfloat16)
        return total + lax.dot_general(
            part, cup_v[:, columns(k)], LAST, preferred_element_type=jnp.float32
        )

    correction = lax.fori_loop(
        0, count, correct, jnp.zeros((low_v.shape[0], border), jnp.float32), unroll=4
    )
    low_v[:, 0:border] = low_v[:, 0:border] - correction
    sol_v[:, 0:size] = upper_block(low_v[...], 0)
    h_buf[me] = jnp.zeros(h_buf.shape[1:], jnp.float32)
    h_buf[me, :, 0:basis] = early + exact(sol_v[:, 0:size], bsub_v[:, 0:size])

    def h_step(k, carry):
        push(h_buf.at[me], h_buf.at[me], H_ALL, device(k))
        return carry

    lax.fori_loop(1, count, h_step, 0)
    drain(g_leaf.at[pl.ds(0, leaves - 1)], recv.at[G_LEAF])
    gram = jnp.sum(g_leaf[...], axis=0)[:, 0:basis]
    drain(s_buf.at[pl.ds(0, fronts - 1)], recv.at[S_ALL])
    drain(h_buf.at[pl.ds(0, count - 1)], recv.at[H_ALL])

    once = jnp.sum(h_buf[...], axis=0)[:, 0:basis]
    rows_cols = (((1,), (0,)), ((), ()))
    both = once + (once - exact(once, gram, rows_cols))
    coef[...] = both
    orth_sub[...] = sol_v[...] - exact(both, bsub_v[...], rows_cols)
    top_sol = jnp.concatenate([s_buf[k] for k in range(fronts)], axis=1)
    orth_sep[...] = top_sol - exact(both, bsep_v[...], rows_cols)

    drain(a_recv, send.at[A_SUM])
    drain(t_buf.at[pl.ds(0, fronts - 1)], send.at[A_ALL])
    drain(b_recv, send.at[B_SUM])
    drain(l_buf.at[pl.ds(0, leaves - 1)], send.at[B_ALL])
    drain(c_recv, send.at[C_SUM])
    drain(s_buf.at[pl.ds(0, fronts - 1)], send.at[S_ALL])
    drain(d_buf.at[pl.ds(0, count - 1)], send.at[D_ALL])
    drain(g_front.at[pl.ds(0, fronts - 1)], send.at[G_FRONT])
    drain(g_leaf.at[pl.ds(0, leaves - 1)], send.at[G_LEAF])
    drain(h_buf.at[pl.ds(0, count - 1)], send.at[H_ALL])


def fused_shards(
    leaves,
    fronts,
    rhs_sub,
    rhs_sep,
    live_rows,
    lower_inv,
    upper_inv,
    couple_low,
    couple_up,
    sep_lower_inv,
    sep_upper_inv,
    basis_sub,
    basis_sep,
):
    vecs, basis = rhs_sub.shape[0], basis_sub.shape[0]
    count = leaves * fronts
    width = rhs_sep.shape[1] // fronts
    size = lower_inv.shape[1]
    full = [
        rhs_sub, rhs_sep, lower_inv, upper_inv, couple_low, couple_up,
        sep_lower_inv, sep_upper_inv, basis_sub, basis_sep,
    ]
    lanes = -(-basis // 128) * 128
    narrow = (2 * vecs, width // 2)

    def wide(*shape):
        return pltpu.VMEM(shape, jnp.float32)

    def slim(slots):
        return pltpu.VMEM((slots,) + narrow, jnp.bfloat16)

    vmem = pl.BlockSpec(memory_space=pltpu.VMEM)
    orth_sub, orth_sep, coef = pl.pallas_call(
        functools.partial(fused, leaves, fronts),
        out_shape=(
            jax.ShapeDtypeStruct(rhs_sub.shape, jnp.float32),
            jax.ShapeDtypeStruct(rhs_sep.shape, jnp.float32),
            jax.ShapeDtypeStruct((vecs, basis), jnp.float32),
        ),
        in_specs=[pl.BlockSpec(memory_space=pltpu.SMEM)]
        + [pl.BlockSpec(memory_space=pl.ANY)] * len(full),
        out_specs=(vmem, vmem, vmem),
        scratch_shapes=[pltpu.VMEM(x.shape, x.dtype) for x in full]
        + [
            wide(vecs, size),
            wide(*rhs_sub.shape),
            slim(count - 1),
            slim(count - 1),
            slim(fronts),
            wide(leaves - 1, vecs, width),
            wide(leaves - 1, vecs, width),
            slim(leaves),
            wide(fronts - 1, vecs, width),
            wide(fronts - 1, vecs, width),
            wide(fronts, vecs, width),
            slim(count),
            wide(fronts, basis, lanes),
            wide(leaves, basis, lanes),
            wide(count, vecs, lanes),
            pltpu.SemaphoreType.DMA((11,)),
            pltpu.SemaphoreType.DMA((10,)),
            pltpu.SemaphoreType.DMA((10,)),
        ],
        compiler_params=pltpu.CompilerParams(
            collective_id=0, has_side_effects=True, vmem_limit_bytes=56 * 1024 * 1024
        ),
    )(live_rows, *full)
    return orth_sub, orth_sep, coef.T


def apply_blocks(vectors, inverse):
    vec_count = vectors.shape[0]
    shaped = vectors.astype(jnp.bfloat16).reshape(vec_count, inverse.shape[0], inverse.shape[1])
    product = jnp.einsum("vkr,krc->vkc", shaped, inverse, preferred_element_type=jnp.float32)
    return product.reshape(vec_count, inverse.shape[0] * inverse.shape[2])


def shards(
    rhs_sub,
    rhs_sep,
    live_rows,
    lower_inv,
    upper_inv,
    couple_low,
    couple_up,
    sep_lower_inv,
    sep_upper_inv,
    basis_sub,
    basis_sep,
):
    vec_count, row_count = rhs_sub.shape
    border = couple_low.shape[0]
    high = lax.Precision.HIGHEST
    live_mask = lax.broadcasted_iota(jnp.int32, (1, row_count), 1) < live_rows[0]
    lower_sol = jnp.where(live_mask, apply_blocks(rhs_sub, lower_inv), 0.0)
    border_rows = lower_sol[:, :border].astype(jnp.bfloat16)
    columns = couple_low
    top_block = lax.psum_scatter(
        lax.dot_general(
            columns, border_rows, (((0,), (1,)), ((), ())), preferred_element_type=jnp.float32
        ),
        "leaf",
        scatter_dimension=0,
        tiled=True,
    )
    top_block = lax.psum(top_block, "front")
    top_rhs = rhs_sep - top_block.T
    lower_part = jnp.dot(
        top_rhs.astype(jnp.bfloat16), sep_lower_inv, preferred_element_type=jnp.float32
    )
    top_lower = lax.psum(lower_part, "leaf")
    upper_part = lax.dot_general(
        top_lower.astype(jnp.bfloat16),
        sep_upper_inv,
        (((1,), (1,)), ((), ())),
        preferred_element_type=jnp.float32,
    )
    top_sol = lax.psum(upper_part, "front")
    columns = couple_up
    correction = lax.dot_general(
        lax.all_gather(top_sol.astype(jnp.bfloat16), "leaf", axis=1, tiled=True),
        columns,
        (((1,), (1,)), ((), ())),
        preferred_element_type=jnp.float32,
    )
    updated = jnp.concatenate([lower_sol[:, :border] - correction, lower_sol[:, border:]], axis=1)
    upper_sol = jnp.where(live_mask, apply_blocks(updated, upper_inv), 0.0)
    coef_sum = jnp.zeros((basis_sub.shape[0], vec_count), jnp.float32)
    for sweep in range(2):
        local_sub = lax.dot_general(basis_sub, upper_sol, (((1,), (1,)), ((), ())), precision=high)
        local_sep = lax.dot_general(basis_sep, top_sol, (((1,), (1,)), ((), ())), precision=high)
        coef_pass = lax.psum(local_sub, ("leaf", "front")) + lax.psum(local_sep, "leaf")
        part_sub = upper_sol
        part_sep = top_sol
        part_sub = part_sub - lax.dot_general(
            coef_pass, basis_sub, (((0,), (0,)), ((), ())), precision=high
        )
        part_sep = part_sep - lax.dot_general(
            coef_pass, basis_sep, (((0,), (0,)), ((), ())), precision=high
        )
        upper_sol = part_sub
        top_sol = part_sep
        coef_sum = coef_sum + coef_pass
    return (upper_sol, top_sol, coef_sum)


def solution(mesh):
    leaves, fronts = mesh.shape["leaf"], mesh.shape["front"]

    def local(*arrays):
        piece = arrays[1].shape[1] // fronts
        if leaves > 1 and fronts > 1 and piece % 256 == 0 and arrays[0].shape[0] == 8:
            return fused_shards(leaves, fronts, *arrays)
        return shards(*arrays)

    return jax.shard_map(
        local,
        mesh=mesh,
        in_specs=(
            P(None, ("leaf", "front")),
            P(None, "leaf"),
            P(("leaf", "front")),
            P(("leaf", "front"), None, None),
            P(("leaf", "front"), None, None),
            P(("leaf", "front"), None),
            P(("leaf", "front"), None),
            P("leaf", "front"),
            P("leaf", "front"),
            P(None, ("leaf", "front")),
            P(None, "leaf"),
        ),
        out_specs=(P(None, ("leaf", "front")), P(None, "leaf"), P()),
        check_vma=False,
    )
```

```python
import functools

import jax
import jax.numpy as jnp
from jax import lax
from jax.experimental import pallas as pl
from jax.experimental.pallas import tpu as pltpu
from jax.sharding import PartitionSpec as P

MESH = pl.DeviceIdType.MESH
HIGH = lax.Precision.HIGHEST
LAST = (((1,), (1,)), ((), ()))
A_PAIR, A_SUM, A_ALL, B_SUM, B_ALL, C_SUM, S_ALL = range(7)
D_ALL, D_PAIR, G_FRONT, G_LEAF, H_FRONT, H_LEAF = range(7, 13)


def fold(piece):
    half = piece.shape[1] // 2
    return jnp.concatenate([piece[:, :half], piece[:, half:]], axis=0)


def unfold(piece):
    piece = piece.astype(jnp.float32)
    rows = piece.shape[0] // 2
    return jnp.concatenate([piece[:rows], piece[rows:]], axis=1)


def exact(left, right, dims=LAST):
    return lax.dot_general(left, right, dims, precision=HIGH, preferred_element_type=jnp.float32)


def flip(index, k):
    bit, result = 1, index
    while bit <= k:
        if k & bit:
            result = result + bit * (1 - 2 * lax.rem(index // bit, 2))
        bit *= 2
    return result


def hand_over(sub, sep, products, orth_sub, orth_sep, coef, held, sems):
    copies = [
        pltpu.make_async_copy(source, target, sems.at[slot])
        for slot, (source, target) in enumerate(
            [(products, held), (sub, orth_sub), (sep, orth_sep)]
        )
    ]
    for copy in copies:
        copy.start()
    copies[0].wait()
    coef[...] = jnp.transpose(held[...])[: coef.shape[0]]
    copies[1].wait()
    copies[2].wait()


def fused(
    leaves,
    fronts,
    live,
    rhs_sub,
    rhs_sep,
    lower_inv,
    upper_inv,
    couple_low,
    couple_up,
    sep_lower,
    sep_upper,
    basis_sub,
    basis_sep,
    orth_sub,
    orth_sep,
    coef,
    rhs_sub_v,
    rhs_sep_v,
    lower_v,
    upper_v,
    clow_v,
    cup_v,
    slow_v,
    sup_v,
    bsub_v,
    bsep_v,
    low_v,
    sol_v,
    a_part,
    a_pair,
    a_send,
    a_recv,
    t_buf,
    b_acc,
    b_send,
    b_recv,
    l_buf,
    c_acc,
    c_send,
    c_recv,
    s_buf,
    d_buf,
    g_front,
    g_leaf,
    h_front,
    h_leaf,
    load,
    send,
    recv,
    recv_pair,
    recv_front,
    recv_leaf,
):
    leaf, front = lax.axis_index("leaf"), lax.axis_index("front")
    half, per_leaf = leaves * fronts // 2, fronts // 2
    parity, place = lax.rem(front, 2), leaf * per_leaf + front // 2
    mate = (leaf, flip(front, 1))
    blocks, size, _ = lower_v.shape
    border = clow_v.shape[0]
    width = s_buf.shape[2]
    basis = bsub_v.shape[0]

    def fetch(source, target, slot):
        return pltpu.make_async_copy(source, target, load.at[slot])

    def push(source, target, step, device, arrived=None):
        pltpu.make_async_remote_copy(
            src_ref=source,
            dst_ref=target,
            send_sem=send.at[step],
            recv_sem=recv.at[step] if arrived is None else arrived,
            device_id=device,
            device_id_type=MESH,
        ).start()

    def drain(view, sem):
        pltpu.make_async_copy(view, view, sem).wait()

    def device(k):
        other = lax.rem(place + k, half)
        return other // per_leaf, 2 * lax.rem(other, per_leaf) + parity

    def columns(index):
        return pl.ds(pl.multiple_of(index * width, width), width)

    first = [
        fetch(rhs_sub, rhs_sub_v, 0),
        fetch(lower_inv.at[pl.ds(0, 1)], lower_v.at[pl.ds(0, 1)], 1),
        fetch(couple_low, clow_v, 2),
    ]
    second = [
        fetch(rhs_sep, rhs_sep_v, 3),
        fetch(lower_inv.at[pl.ds(1, blocks - 1)], lower_v.at[pl.ds(1, blocks - 1)], 4),
        fetch(upper_inv, upper_v, 5),
        fetch(basis_sub, bsub_v, 6),
        fetch(basis_sep, bsep_v, 7),
    ]
    third = [fetch(sep_lower, slow_v, 8), fetch(sep_upper, sup_v, 9), fetch(couple_up, cup_v, 10)]
    for copy in first:
        copy.start()

    barrier = pltpu.get_barrier_semaphore()

    def greet(k, carry):
        pl.semaphore_signal(barrier, inc=1, device_id=device(k), device_id_type=MESH)
        return carry

    lax.fori_loop(1, half, greet, 0)
    for k in range(1, fronts, 2):
        pl.semaphore_signal(
            barrier, inc=1, device_id=(leaf, flip(front, k)), device_id_type=MESH
        )
    for copy in second:
        copy.start()

    def live_part(value, k):
        row = lax.broadcasted_iota(jnp.int32, value.shape, 1) + k * size
        return jnp.where(row < live[0], value, 0.0)

    def lower_block(k):
        part = rhs_sub_v[:, k * size : (k + 1) * size].astype(jnp.bfloat16)
        return live_part(jnp.dot(part, lower_v[k], preferred_element_type=jnp.float32), k)

    def upper_block(value, k):
        part = value.astype(jnp.bfloat16)
        return live_part(jnp.dot(part, upper_v[k], preferred_element_type=jnp.float32), k)

    first[0].wait()
    first[1].wait()
    low_v[...] = lower_block(0)
    border_rows = low_v[:, :border].astype(jnp.bfloat16)
    first[2].wait()
    for copy in third:
        copy.start()

    greeted = False
    for group in range(2):
        ahead, some = group * (half // 2), half // 2
        for q in range(ahead, ahead + some):
            for p in range(2):
                at = (2 * q + p) * width
                a_part[p, q] = jnp.dot(
                    border_rows, clow_v[:, at : at + width], preferred_element_type=jnp.float32
                )
        if not greeted:
            pl.semaphore_wait(barrier, half - 1 + fronts // 2)
            greeted = True
        push(
            a_part.at[1 - parity, pl.ds(ahead, some)],
            a_pair.at[pl.ds(ahead, some)],
            A_PAIR,
            mate,
            recv_pair.at[group],
        )
    second[0].wait()
    for group in range(2):
        ahead, some = group * (half // 2), half // 2
        drain(a_pair.at[pl.ds(ahead, some)], recv_pair.at[group])
        for q in range(ahead, ahead + some):
            a_send[q] = fold(a_part[parity, q] + a_pair[q]).astype(jnp.bfloat16)

    def a_step(k, carry):
        push(a_send.at[lax.rem(place + k, half)], a_recv.at[k - 1], A_SUM, device(k))
        return carry

    lax.fori_loop(1, half, a_step, 0)

    second[3].wait()
    second[4].wait()
    own = bsep_v[:, columns(front)]
    gram = exact(bsub_v[...], bsub_v[...]) + exact(own, own)
    g_front[front] = jnp.zeros(g_front.shape[1:], jnp.float32)
    g_front[front, :, 0:basis] = gram
    for k in range(1, fronts):
        push(g_front.at[front], g_front.at[front], G_FRONT, (leaf, flip(front, k)))
    top = rhs_sep_v[:, columns(front)] - (a_part[parity, place] + a_pair[place])

    drain(a_recv, recv.at[A_SUM])
    top = fold(top) - jnp.sum(a_recv[...].astype(jnp.float32), axis=0)
    t_buf[0] = top.astype(jnp.bfloat16)
    for k in range(fronts - 1, 0, -1):
        push(t_buf.at[0], t_buf.at[k], A_ALL, (leaf, flip(front, k)), recv_front.at[k])

    def strip(index):
        return pl.ds(pl.multiple_of(index * width, width), width)

    def top_piece(k):
        if k:
            drain(t_buf.at[k], recv_front.at[k])
        return unfold(t_buf[k]).astype(jnp.bfloat16), strip(flip(front, k))

    def times_lower(piece, to):
        return jnp.dot(piece[0], slow_v[piece[1], to], preferred_element_type=jnp.float32)

    third[0].wait()
    for k in range(fronts - 2):
        piece = top_piece(k)
        for n in range(leaves):
            product = times_lower(piece, slice(n * width, (n + 1) * width))
            b_acc[n] = b_acc[n] + product if k else product
        if k == 0:
            drain(g_front.at[pl.ds(0, fronts - 1)], recv.at[G_FRONT])
            g_leaf[leaf] = jnp.sum(g_front[...], axis=0)
            for j in range(1, leaves):
                push(g_leaf.at[leaf], g_leaf.at[leaf], G_LEAF, (flip(leaf, j), front))
    last = [top_piece(k) for k in range(fronts - 2, fronts)]

    def lower_piece(to):
        return b_acc[to] + sum(times_lower(piece, columns(to)) for piece in last)

    for k in range(leaves - 1, 0, -1):
        to = flip(leaf, k)
        b_send[k - 1] = lower_piece(to)
        push(b_send.at[k - 1], b_recv.at[k - 1], B_SUM, (to, front))
    piece = lower_piece(leaf)
    drain(b_recv, recv.at[B_SUM])
    piece = piece + jnp.sum(b_recv[...], axis=0)
    l_buf[0] = fold(piece).astype(jnp.bfloat16)
    for k in range(leaves - 1, 0, -1):
        push(l_buf.at[0], l_buf.at[k], B_ALL, (flip(leaf, k), front), recv_leaf.at[k])

    def low_piece(k):
        if k:
            drain(l_buf.at[k], recv_leaf.at[k])
        return unfold(l_buf[k]).astype(jnp.bfloat16), columns(flip(leaf, k))

    def times_upper(piece, to):
        return lax.dot_general(
            piece[0], sup_v[to, piece[1]], LAST, preferred_element_type=jnp.float32
        )

    third[1].wait()
    for k in range(leaves - 2):
        piece = low_piece(k)
        for n in range(fronts):
            product = times_upper(piece, slice(n * width, (n + 1) * width))
            c_acc[n] = c_acc[n] + product if k else product
    last2 = [low_piece(k) for k in range(leaves - 2, leaves)]

    def upper_piece(to):
        return c_acc[to] + sum(times_upper(piece, strip(to)) for piece in last2)

    for k in range(fronts - 1, 0, -1):
        to = flip(front, k)
        c_send[k - 1] = upper_piece(to)
        push(c_send.at[k - 1], c_recv.at[k - 1], C_SUM, (leaf, to))
    piece = upper_piece(front)
    drain(c_recv, recv.at[C_SUM])
    piece = piece + jnp.sum(c_recv[...], axis=0)

    d_buf[parity, place] = fold(piece).astype(jnp.bfloat16)
    mine = d_buf.at[parity, place]

    def d_step(k, carry):
        push(mine, mine, D_ALL, device(k))
        return carry

    lax.fori_loop(1, half, d_step, 0)
    s_buf[front] = piece
    for k in range(1, fronts):
        push(s_buf.at[front], s_buf.at[front], S_ALL, (leaf, flip(front, k)))

    second[1].wait()
    second[2].wait()
    for k in range(1, blocks):
        sol_v[:, k * size : (k + 1) * size] = upper_block(lower_block(k), k)
    early = exact(sol_v[:, size:], bsub_v[:, size:]) + exact(piece, bsep_v[:, columns(front)])
    third[2].wait()

    def correct(p):
        return sum(
            lax.dot_general(
                unfold(d_buf[p, q]).astype(jnp.bfloat16),
                cup_v[:, columns(2 * q + p)],
                LAST,
                preferred_element_type=jnp.float32,
            )
            for q in range(half)
        )

    drain(d_buf.at[0, pl.ds(0, half - 1)], recv.at[D_ALL])
    push(d_buf.at[parity], d_buf.at[parity], D_PAIR, mate)
    correction = correct(parity)
    drain(d_buf.at[0], recv.at[D_PAIR])
    correction = correction + correct(1 - parity)
    low_v[:, 0:border] = low_v[:, 0:border] - correction
    sol_v[:, 0:size] = upper_block(low_v[...], 0)
    h_front[front] = jnp.zeros(h_front.shape[1:], jnp.float32)
    h_front[front, :, 0:basis] = early + exact(sol_v[:, 0:size], bsub_v[:, 0:size])
    for k in range(fronts - 1, 0, -1):
        push(h_front.at[front], h_front.at[front], H_FRONT, (leaf, flip(front, k)))
    drain(g_leaf.at[pl.ds(0, leaves - 1)], recv.at[G_LEAF])
    gram = jnp.sum(g_leaf[...], axis=0)[:, 0:basis]
    drain(h_front.at[pl.ds(0, fronts - 1)], recv.at[H_FRONT])
    h_leaf[leaf] = jnp.sum(h_front[...], axis=0)
    for k in range(leaves - 1, 0, -1):
        push(h_leaf.at[leaf], h_leaf.at[leaf], H_LEAF, (flip(leaf, k), front))
    drain(s_buf.at[pl.ds(0, fronts - 1)], recv.at[S_ALL])
    drain(h_leaf.at[pl.ds(0, leaves - 1)], recv.at[H_LEAF])

    once = jnp.sum(h_leaf[...], axis=0)[:, 0:basis]
    rows_cols = (((1,), (0,)), ((), ()))
    both = once + (once - exact(once, gram, rows_cols))
    coef[...] = jnp.zeros(coef.shape, jnp.float32)
    coef[:, 0:basis] = both
    orth_sub[...] = sol_v[...] - exact(both, bsub_v[...], rows_cols)
    top_sol = jnp.concatenate([s_buf[k] for k in range(fronts)], axis=1)
    orth_sep[...] = top_sol - exact(both, bsep_v[...], rows_cols)

    drain(a_pair, send.at[A_PAIR])
    drain(a_recv, send.at[A_SUM])
    drain(t_buf.at[pl.ds(0, fronts - 1)], send.at[A_ALL])
    drain(b_recv, send.at[B_SUM])
    drain(l_buf.at[pl.ds(0, leaves - 1)], send.at[B_ALL])
    drain(c_recv, send.at[C_SUM])
    drain(s_buf.at[pl.ds(0, fronts - 1)], send.at[S_ALL])
    drain(d_buf.at[0, pl.ds(0, half - 1)], send.at[D_ALL])
    drain(d_buf.at[0], send.at[D_PAIR])
    drain(g_front.at[pl.ds(0, fronts - 1)], send.at[G_FRONT])
    drain(g_leaf.at[pl.ds(0, leaves - 1)], send.at[G_LEAF])
    drain(h_front.at[pl.ds(0, fronts - 1)], send.at[H_FRONT])
    drain(h_leaf.at[pl.ds(0, leaves - 1)], send.at[H_LEAF])


def fused_shards(
    leaves,
    fronts,
    rhs_sub,
    rhs_sep,
    live_rows,
    lower_inv,
    upper_inv,
    couple_low,
    couple_up,
    sep_lower_inv,
    sep_upper_inv,
    basis_sub,
    basis_sep,
):
    vecs, basis = rhs_sub.shape[0], basis_sub.shape[0]
    half = leaves * fronts // 2
    width = rhs_sep.shape[1] // fronts
    size = lower_inv.shape[1]
    full = [
        rhs_sub, rhs_sep, lower_inv, upper_inv, couple_low, couple_up,
        sep_lower_inv, sep_upper_inv, basis_sub, basis_sep,
    ]
    lanes = -(-basis // 128) * 128
    narrow = (2 * vecs, width // 2)

    def wide(*shape):
        return pltpu.VMEM(shape, jnp.float32)

    def slim(slots):
        return pltpu.VMEM((slots,) + narrow, jnp.bfloat16)

    vmem = pl.BlockSpec(memory_space=pltpu.VMEM)
    anywhere = pl.BlockSpec(memory_space=pl.ANY)
    parts = pl.pallas_call(
        functools.partial(fused, leaves, fronts),
        out_shape=(
            jax.ShapeDtypeStruct(rhs_sub.shape, jnp.float32),
            jax.ShapeDtypeStruct(rhs_sep.shape, jnp.float32),
            jax.ShapeDtypeStruct((vecs, lanes), jnp.float32),
        ),
        in_specs=[pl.BlockSpec(memory_space=pltpu.SMEM)]
        + [pl.BlockSpec(memory_space=pl.ANY)] * len(full),
        out_specs=(vmem, vmem, vmem),
        scratch_shapes=[pltpu.VMEM(x.shape, x.dtype) for x in full]
        + [
            wide(vecs, size),
            wide(*rhs_sub.shape),
            wide(2, half, vecs, width),
            wide(half, vecs, width),
            slim(half),
            slim(half - 1),
            slim(fronts),
            wide(leaves, vecs, width),
            wide(leaves - 1, vecs, width),
            wide(leaves - 1, vecs, width),
            slim(leaves),
            wide(fronts, vecs, width),
            wide(fronts - 1, vecs, width),
            wide(fronts - 1, vecs, width),
            wide(fronts, vecs, width),
            pltpu.VMEM((2, half) + narrow, jnp.bfloat16),
            wide(fronts, basis, lanes),
            wide(leaves, basis, lanes),
            wide(fronts, vecs, lanes),
            wide(leaves, vecs, lanes),
            pltpu.SemaphoreType.DMA((11,)),
            pltpu.SemaphoreType.DMA((13,)),
            pltpu.SemaphoreType.DMA((13,)),
            pltpu.SemaphoreType.DMA((2,)),
            pltpu.SemaphoreType.DMA((fronts,)),
            pltpu.SemaphoreType.DMA((leaves,)),
        ],
        compiler_params=pltpu.CompilerParams(
            collective_id=0, has_side_effects=True, vmem_limit_bytes=56 * 1024 * 1024
        ),
    )(live_rows, *full)
    return pl.pallas_call(
        hand_over,
        out_shape=(
            jax.ShapeDtypeStruct(rhs_sub.shape, jnp.float32),
            jax.ShapeDtypeStruct(rhs_sep.shape, jnp.float32),
            jax.ShapeDtypeStruct((basis, vecs), jnp.float32),
        ),
        in_specs=[anywhere] * 3,
        out_specs=(anywhere, anywhere, vmem),
        scratch_shapes=[wide(vecs, lanes), pltpu.SemaphoreType.DMA((3,))],
        compiler_params=pltpu.CompilerParams(vmem_limit_bytes=56 * 1024 * 1024),
    )(*parts)


def apply_blocks(vectors, inverse):
    vec_count = vectors.shape[0]
    shaped = vectors.astype(jnp.bfloat16).reshape(vec_count, inverse.shape[0], inverse.shape[1])
    product = jnp.einsum("vkr,krc->vkc", shaped, inverse, preferred_element_type=jnp.float32)
    return product.reshape(vec_count, inverse.shape[0] * inverse.shape[2])


def shards(
    rhs_sub,
    rhs_sep,
    live_rows,
    lower_inv,
    upper_inv,
    couple_low,
    couple_up,
    sep_lower_inv,
    sep_upper_inv,
    basis_sub,
    basis_sep,
):
    vec_count, row_count = rhs_sub.shape
    border = couple_low.shape[0]
    high = lax.Precision.HIGHEST
    live_mask = lax.broadcasted_iota(jnp.int32, (1, row_count), 1) < live_rows[0]
    lower_sol = jnp.where(live_mask, apply_blocks(rhs_sub, lower_inv), 0.0)
    border_rows = lower_sol[:, :border].astype(jnp.bfloat16)
    columns = couple_low
    top_block = lax.psum_scatter(
        lax.dot_general(
            columns, border_rows, (((0,), (1,)), ((), ())), preferred_element_type=jnp.float32
        ),
        "leaf",
        scatter_dimension=0,
        tiled=True,
    )
    top_block = lax.psum(top_block, "front")
    top_rhs = rhs_sep - top_block.T
    lower_part = jnp.dot(
        top_rhs.astype(jnp.bfloat16), sep_lower_inv, preferred_element_type=jnp.float32
    )
    top_lower = lax.psum(lower_part, "leaf")
    upper_part = lax.dot_general(
        top_lower.astype(jnp.bfloat16),
        sep_upper_inv,
        (((1,), (1,)), ((), ())),
        preferred_element_type=jnp.float32,
    )
    top_sol = lax.psum(upper_part, "front")
    columns = couple_up
    correction = lax.dot_general(
        lax.all_gather(top_sol.astype(jnp.bfloat16), "leaf", axis=1, tiled=True),
        columns,
        (((1,), (1,)), ((), ())),
        preferred_element_type=jnp.float32,
    )
    updated = jnp.concatenate([lower_sol[:, :border] - correction, lower_sol[:, border:]], axis=1)
    upper_sol = jnp.where(live_mask, apply_blocks(updated, upper_inv), 0.0)
    coef_sum = jnp.zeros((basis_sub.shape[0], vec_count), jnp.float32)
    for sweep in range(2):
        local_sub = lax.dot_general(basis_sub, upper_sol, (((1,), (1,)), ((), ())), precision=high)
        local_sep = lax.dot_general(basis_sep, top_sol, (((1,), (1,)), ((), ())), precision=high)
        coef_pass = lax.psum(local_sub, ("leaf", "front")) + lax.psum(local_sep, "leaf")
        part_sub = upper_sol
        part_sep = top_sol
        part_sub = part_sub - lax.dot_general(
            coef_pass, basis_sub, (((0,), (0,)), ((), ())), precision=high
        )
        part_sep = part_sep - lax.dot_general(
            coef_pass, basis_sep, (((0,), (0,)), ((), ())), precision=high
        )
        upper_sol = part_sub
        top_sol = part_sep
        coef_sum = coef_sum + coef_pass
    return (upper_sol, top_sol, coef_sum)


def solution(mesh):
    leaves, fronts = mesh.shape["leaf"], mesh.shape["front"]

    def local(*arrays):
        piece = arrays[1].shape[1] // fronts
        paired = leaves > 2 and fronts > 2 and not (leaves & (leaves - 1) or fronts & (fronts - 1))
        if paired and piece % 256 == 0 and arrays[0].shape[0] == 8:
            return fused_shards(leaves, fronts, *arrays)
        return shards(*arrays)

    return jax.shard_map(
        local,
        mesh=mesh,
        in_specs=(
            P(None, ("leaf", "front")),
            P(None, "leaf"),
            P(("leaf", "front")),
            P(("leaf", "front"), None, None),
            P(("leaf", "front"), None, None),
            P(("leaf", "front"), None),
            P(("leaf", "front"), None),
            P("leaf", "front"),
            P("leaf", "front"),
            P(None, ("leaf", "front")),
            P(None, "leaf"),
        ),
        out_specs=(P(None, ("leaf", "front")), P(None, "leaf"), P()),
        check_vma=False,
    )
```

```python
import functools

import jax
import jax.numpy as jnp
from jax import lax
from jax.experimental import pallas as pl
from jax.experimental.pallas import tpu as pltpu
from jax.sharding import PartitionSpec as P

MESH = pl.DeviceIdType.MESH
HIGH = lax.Precision.HIGHEST
LAST = (((1,), (1,)), ((), ()))
A_PAIR, A_SUM, A_ALL, B_SUM, B_ALL, C_SUM, S_ALL = range(7)
D_ALL, D_PAIR, G_FRONT, G_LEAF, H_FRONT, H_LEAF = range(7, 13)


def fold(piece):
    half = piece.shape[1] // 2
    return jnp.concatenate([piece[:, :half], piece[:, half:]], axis=0)


def unfold(piece):
    piece = piece.astype(jnp.float32)
    rows = piece.shape[0] // 2
    return jnp.concatenate([piece[:rows], piece[rows:]], axis=1)


def exact(left, right, dims=LAST):
    return lax.dot_general(left, right, dims, precision=HIGH, preferred_element_type=jnp.float32)


def flip(index, k):
    bit, result = 1, index
    while bit <= k:
        if k & bit:
            result = result + bit * (1 - 2 * lax.rem(index // bit, 2))
        bit *= 2
    return result


def hand_over(*refs):
    given, placed, held, (into, out) = refs[:3], refs[3:6], refs[6:9], refs[9:]
    reads = [pltpu.make_async_copy(given[k], held[k], into.at[k]) for k in range(3)]
    writes = [pltpu.make_async_copy(held[k], placed[k], out.at[k]) for k in range(3)]
    for copy in reads:
        copy.start()
    for read, write in zip(reads, writes):
        read.wait()
        write.start()
    for copy in writes:
        copy.wait()


def fused(
    leaves,
    fronts,
    live_rows,
    rhs_sub,
    rhs_sep,
    lower_inv,
    upper_inv,
    couple_low,
    couple_up,
    sep_lower,
    sep_upper,
    basis_sub,
    basis_sep,
    orth_sub,
    orth_sep,
    coef,
    rhs_sub_v,
    rhs_sep_v,
    lower_v,
    upper_v,
    clow_v,
    cup_v,
    slow_v,
    sup_v,
    bsub_v,
    bsep_v,
    low_v,
    sol_v,
    a_part,
    a_pair,
    a_send,
    a_recv,
    t_buf,
    b_acc,
    b_send,
    b_recv,
    l_buf,
    c_acc,
    c_send,
    c_recv,
    s_buf,
    d_buf,
    g_front,
    g_leaf,
    h_front,
    h_leaf,
    load,
    send,
    recv,
    recv_pair,
    recv_front,
    recv_leaf,
    live,
):
    leaf, front = lax.axis_index("leaf"), lax.axis_index("front")
    half, per_leaf = leaves * fronts // 2, fronts // 2
    parity, place = lax.rem(front, 2), leaf * per_leaf + front // 2
    mate = (leaf, flip(front, 1))
    blocks, size, _ = lower_v.shape
    border = clow_v.shape[0]
    width = s_buf.shape[2]
    basis = bsub_v.shape[0]

    def fetch(source, target, slot):
        return pltpu.make_async_copy(source, target, load.at[slot])

    def push(source, target, step, device, arrived=None):
        pltpu.make_async_remote_copy(
            src_ref=source,
            dst_ref=target,
            send_sem=send.at[step],
            recv_sem=recv.at[step] if arrived is None else arrived,
            device_id=device,
            device_id_type=MESH,
        ).start()

    def drain(view, sem):
        pltpu.make_async_copy(view, view, sem).wait()

    def device(k):
        return flip(leaf, k // per_leaf), flip(front, 2 * (k % per_leaf))

    def columns(index):
        return pl.ds(pl.multiple_of(index * width, width), width)

    first = [
        fetch(rhs_sub, rhs_sub_v, 0),
        fetch(lower_inv.at[pl.ds(0, 1)], lower_v.at[pl.ds(0, 1)], 1),
        fetch(couple_low, clow_v, 2),
        fetch(live_rows, live, 11),
    ]
    second = [
        fetch(rhs_sep, rhs_sep_v, 3),
        fetch(lower_inv.at[pl.ds(1, blocks - 1)], lower_v.at[pl.ds(1, blocks - 1)], 4),
        fetch(upper_inv, upper_v, 5),
        fetch(basis_sub, bsub_v, 6),
        fetch(basis_sep, bsep_v, 7),
    ]

    def fetch_rows(source, target, slot):
        rows = source.shape[0] // 4
        for k in range(4):
            some = pl.ds(k * rows, rows)
            fetch(source.at[some], target.at[some], slot).start()

    for copy in first:
        copy.start()

    barrier = pltpu.get_barrier_semaphore()

    for k in range(1, half):
        pl.semaphore_signal(barrier, inc=1, device_id=device(k), device_id_type=MESH)
    for k in range(1, fronts, 2):
        pl.semaphore_signal(
            barrier, inc=1, device_id=(leaf, flip(front, k)), device_id_type=MESH
        )
    for copy in second:
        copy.start()

    def live_part(value, k):
        row = lax.broadcasted_iota(jnp.int32, value.shape, 1) + k * size
        return jnp.where(row < live[0], value, 0.0)

    def lower_block(k):
        part = rhs_sub_v[:, k * size : (k + 1) * size].astype(jnp.bfloat16)
        return live_part(jnp.dot(part, lower_v[k], preferred_element_type=jnp.float32), k)

    def upper_block(value, k):
        part = value.astype(jnp.bfloat16)
        return live_part(jnp.dot(part, upper_v[k], preferred_element_type=jnp.float32), k)

    first[0].wait()
    first[1].wait()
    first[3].wait()
    low_v[...] = lower_block(0)
    border_rows = low_v[:, :border].astype(jnp.bfloat16)
    first[2].wait()
    fetch_rows(sep_lower, slow_v, 8)

    greeted = False
    for group in range(2):
        ahead, some = group * (half // 2), half // 2
        for q in range(ahead, ahead + some):
            for p in range(2):
                at = (2 * q + p) * width
                a_part[p, q] = jnp.dot(
                    border_rows, clow_v[:, at : at + width], preferred_element_type=jnp.float32
                )
        if not greeted:
            pl.semaphore_wait(barrier, half - 1 + fronts // 2)
            greeted = True
        push(
            a_part.at[1 - parity, pl.ds(ahead, some)],
            a_pair.at[pl.ds(ahead, some)],
            A_PAIR,
            mate,
            recv_pair.at[group],
        )
    second[0].wait()
    for group in range(2):
        ahead, some = group * (half // 2), half // 2
        drain(a_pair.at[pl.ds(ahead, some)], recv_pair.at[group])
        for q in range(ahead, ahead + some):
            a_send[q] = fold(a_part[parity, q] + a_pair[q]).astype(jnp.bfloat16)

    for k in range(half - 1, 0, -1):
        push(a_send.at[flip(place, k)], a_recv.at[k - 1], A_SUM, device(k))

    second[3].wait()
    second[4].wait()
    own = bsep_v[:, columns(front)]
    gram = exact(bsub_v[...], bsub_v[...]) + exact(own, own)
    g_front[front] = jnp.zeros(g_front.shape[1:], jnp.float32)
    g_front[front, :, 0:basis] = gram
    for k in range(1, fronts):
        push(g_front.at[front], g_front.at[front], G_FRONT, (leaf, flip(front, k)))
    top = rhs_sep_v[:, columns(front)] - (a_part[parity, place] + a_pair[place])

    drain(a_recv, recv.at[A_SUM])
    top = fold(top) - jnp.sum(a_recv[...].astype(jnp.float32), axis=0)
    t_buf[0] = top.astype(jnp.bfloat16)
    for k in range(fronts - 1, 0, -1):
        push(t_buf.at[0], t_buf.at[k], A_ALL, (leaf, flip(front, k)), recv_front.at[k])

    def strip(index):
        return pl.ds(pl.multiple_of(index * width, width), width)

    def top_piece(k):
        if k:
            drain(t_buf.at[k], recv_front.at[k])
        return unfold(t_buf[k]).astype(jnp.bfloat16), strip(flip(front, k))

    def times_lower(piece, to):
        return jnp.dot(piece[0], slow_v[piece[1], to], preferred_element_type=jnp.float32)

    drain(slow_v, load.at[8])
    fetch_rows(sep_upper, sup_v, 9)
    fetch(couple_up, cup_v, 10).start()
    for k in range(fronts - 2):
        piece = top_piece(k)
        for n in range(leaves):
            product = times_lower(piece, slice(n * width, (n + 1) * width))
            b_acc[n] = b_acc[n] + product if k else product
        if k == 0:
            drain(g_front.at[pl.ds(0, fronts - 1)], recv.at[G_FRONT])
            g_leaf[leaf] = jnp.sum(g_front[...], axis=0)
            for j in range(1, leaves):
                push(g_leaf.at[leaf], g_leaf.at[leaf], G_LEAF, (flip(leaf, j), front))
    last = [top_piece(k) for k in range(fronts - 2, fronts)]

    def lower_piece(to):
        return b_acc[to] + sum(times_lower(piece, columns(to)) for piece in last)

    for k in range(leaves - 1, 0, -1):
        to = flip(leaf, k)
        b_send[k - 1] = lower_piece(to)
        push(b_send.at[k - 1], b_recv.at[k - 1], B_SUM, (to, front))
    piece = lower_piece(leaf)
    drain(b_recv, recv.at[B_SUM])
    piece = piece + jnp.sum(b_recv[...], axis=0)
    l_buf[0] = fold(piece).astype(jnp.bfloat16)
    for k in range(leaves - 1, 0, -1):
        push(l_buf.at[0], l_buf.at[k], B_ALL, (flip(leaf, k), front), recv_leaf.at[k])

    def low_piece(k):
        if k:
            drain(l_buf.at[k], recv_leaf.at[k])
        return unfold(l_buf[k]).astype(jnp.bfloat16), columns(flip(leaf, k))

    def times_upper(piece, to):
        return lax.dot_general(
            piece[0], sup_v[to, piece[1]], LAST, preferred_element_type=jnp.float32
        )

    drain(sup_v, load.at[9])
    for k in range(leaves - 2):
        piece = low_piece(k)
        for n in range(fronts):
            product = times_upper(piece, slice(n * width, (n + 1) * width))
            c_acc[n] = c_acc[n] + product if k else product
    last2 = [low_piece(k) for k in range(leaves - 2, leaves)]

    def upper_piece(to):
        return c_acc[to] + sum(times_upper(piece, strip(to)) for piece in last2)

    for k in range(fronts - 1, 0, -1):
        to = flip(front, k)
        c_send[k - 1] = upper_piece(to)
        push(c_send.at[k - 1], c_recv.at[k - 1], C_SUM, (leaf, to))
    piece = upper_piece(front)
    drain(c_recv, recv.at[C_SUM])
    piece = piece + jnp.sum(c_recv[...], axis=0)

    d_buf[parity, place] = fold(piece).astype(jnp.bfloat16)
    mine = d_buf.at[parity, place]

    for k in range(half - 1, 0, -1):
        push(mine, mine, D_ALL, device(k))
    s_buf[front] = piece
    for k in range(1, fronts):
        push(s_buf.at[front], s_buf.at[front], S_ALL, (leaf, flip(front, k)))

    second[1].wait()
    second[2].wait()
    for k in range(1, blocks):
        sol_v[:, k * size : (k + 1) * size] = upper_block(lower_block(k), k)
    early = exact(sol_v[:, size:], bsub_v[:, size:]) + exact(piece, bsep_v[:, columns(front)])
    drain(cup_v, load.at[10])

    def correct(p):
        return sum(
            lax.dot_general(
                unfold(d_buf[p, q]).astype(jnp.bfloat16),
                cup_v[:, columns(2 * q + p)],
                LAST,
                preferred_element_type=jnp.float32,
            )
            for q in range(half)
        )

    drain(d_buf.at[0, pl.ds(0, half - 1)], recv.at[D_ALL])
    push(d_buf.at[parity], d_buf.at[parity], D_PAIR, mate)
    correction = correct(parity)
    drain(d_buf.at[0], recv.at[D_PAIR])
    correction = correction + correct(1 - parity)
    low_v[:, 0:border] = low_v[:, 0:border] - correction
    sol_v[:, 0:size] = upper_block(low_v[...], 0)
    h_front[front] = jnp.zeros(h_front.shape[1:], jnp.float32)
    h_front[front, :, 0:basis] = early + exact(sol_v[:, 0:size], bsub_v[:, 0:size])
    for k in range(fronts - 1, 0, -1):
        push(h_front.at[front], h_front.at[front], H_FRONT, (leaf, flip(front, k)))
    drain(g_leaf.at[pl.ds(0, leaves - 1)], recv.at[G_LEAF])
    gram = jnp.sum(g_leaf[...], axis=0)[:, 0:basis]
    drain(h_front.at[pl.ds(0, fronts - 1)], recv.at[H_FRONT])
    h_leaf[leaf] = jnp.sum(h_front[...], axis=0)
    for k in range(leaves - 1, 0, -1):
        push(h_leaf.at[leaf], h_leaf.at[leaf], H_LEAF, (flip(leaf, k), front))
    drain(s_buf.at[pl.ds(0, fronts - 1)], recv.at[S_ALL])
    drain(h_leaf.at[pl.ds(0, leaves - 1)], recv.at[H_LEAF])

    once = jnp.sum(h_leaf[...], axis=0)[:, 0:basis]
    rows_cols = (((1,), (0,)), ((), ()))
    both = once + (once - exact(once, gram, rows_cols))
    coef[...] = both
    orth_sub[...] = sol_v[...] - exact(both, bsub_v[...], rows_cols)
    top_sol = jnp.concatenate([s_buf[k] for k in range(fronts)], axis=1)
    orth_sep[...] = top_sol - exact(both, bsep_v[...], rows_cols)

    drain(a_pair, send.at[A_PAIR])
    drain(a_recv, send.at[A_SUM])
    drain(t_buf.at[pl.ds(0, fronts - 1)], send.at[A_ALL])
    drain(b_recv, send.at[B_SUM])
    drain(l_buf.at[pl.ds(0, leaves - 1)], send.at[B_ALL])
    drain(c_recv, send.at[C_SUM])
    drain(s_buf.at[pl.ds(0, fronts - 1)], send.at[S_ALL])
    drain(d_buf.at[0, pl.ds(0, half - 1)], send.at[D_ALL])
    drain(d_buf.at[0], send.at[D_PAIR])
    drain(g_front.at[pl.ds(0, fronts - 1)], send.at[G_FRONT])
    drain(g_leaf.at[pl.ds(0, leaves - 1)], send.at[G_LEAF])
    drain(h_front.at[pl.ds(0, fronts - 1)], send.at[H_FRONT])
    drain(h_leaf.at[pl.ds(0, leaves - 1)], send.at[H_LEAF])


def fused_shards(
    leaves,
    fronts,
    rhs_sub,
    rhs_sep,
    live_rows,
    lower_inv,
    upper_inv,
    couple_low,
    couple_up,
    sep_lower_inv,
    sep_upper_inv,
    basis_sub,
    basis_sep,
):
    vecs, basis = rhs_sub.shape[0], basis_sub.shape[0]
    half = leaves * fronts // 2
    width = rhs_sep.shape[1] // fronts
    size = lower_inv.shape[1]
    full = [
        rhs_sub, rhs_sep, lower_inv, upper_inv, couple_low, couple_up,
        sep_lower_inv, sep_upper_inv, basis_sub, basis_sep,
    ]
    lanes = -(-basis // 128) * 128
    narrow = (2 * vecs, width // 2)

    def wide(*shape):
        return pltpu.VMEM(shape, jnp.float32)

    def slim(slots):
        return pltpu.VMEM((slots,) + narrow, jnp.bfloat16)

    vmem = pl.BlockSpec(memory_space=pltpu.VMEM)
    anywhere = pl.BlockSpec(memory_space=pltpu.HBM)
    parts = pl.pallas_call(
        functools.partial(fused, leaves, fronts),
        out_shape=(
            jax.ShapeDtypeStruct(rhs_sub.shape, jnp.float32),
            jax.ShapeDtypeStruct(rhs_sep.shape, jnp.float32),
            jax.ShapeDtypeStruct((vecs, basis), jnp.float32),
        ),
        in_specs=[anywhere] * (len(full) + 1),
        out_specs=(vmem, vmem, vmem),
        scratch_shapes=[pltpu.VMEM(x.shape, x.dtype) for x in full]
        + [
            wide(vecs, size),
            wide(*rhs_sub.shape),
            wide(2, half, vecs, width),
            wide(half, vecs, width),
            slim(half),
            slim(half - 1),
            slim(fronts),
            wide(leaves, vecs, width),
            wide(leaves - 1, vecs, width),
            wide(leaves - 1, vecs, width),
            slim(leaves),
            wide(fronts, vecs, width),
            wide(fronts - 1, vecs, width),
            wide(fronts - 1, vecs, width),
            wide(fronts, vecs, width),
            pltpu.VMEM((2, half) + narrow, jnp.bfloat16),
            wide(fronts, basis, lanes),
            wide(leaves, basis, lanes),
            wide(fronts, vecs, lanes),
            wide(leaves, vecs, lanes),
            pltpu.SemaphoreType.DMA((12,)),
            pltpu.SemaphoreType.DMA((13,)),
            pltpu.SemaphoreType.DMA((13,)),
            pltpu.SemaphoreType.DMA((2,)),
            pltpu.SemaphoreType.DMA((fronts,)),
            pltpu.SemaphoreType.DMA((leaves,)),
            pltpu.SMEM(live_rows.shape, jnp.int32),
        ],
        compiler_params=pltpu.CompilerParams(
            collective_id=0, has_side_effects=True, vmem_limit_bytes=56 * 1024 * 1024
        ),
    )(live_rows, *full)
    orth_sub, orth_sep, coef = pl.pallas_call(
        hand_over,
        out_shape=tuple(jax.ShapeDtypeStruct(x.shape, x.dtype) for x in parts),
        in_specs=[anywhere] * 3,
        out_specs=(anywhere,) * 3,
        scratch_shapes=[pltpu.VMEM(x.shape, x.dtype) for x in parts]
        + [pltpu.SemaphoreType.DMA((3,))] * 2,
        compiler_params=pltpu.CompilerParams(vmem_limit_bytes=56 * 1024 * 1024),
    )(*parts)
    return orth_sub, orth_sep, coef.T


def apply_blocks(vectors, inverse):
    vec_count = vectors.shape[0]
    shaped = vectors.astype(jnp.bfloat16).reshape(vec_count, inverse.shape[0], inverse.shape[1])
    product = jnp.einsum("vkr,krc->vkc", shaped, inverse, preferred_element_type=jnp.float32)
    return product.reshape(vec_count, inverse.shape[0] * inverse.shape[2])


def shards(
    rhs_sub,
    rhs_sep,
    live_rows,
    lower_inv,
    upper_inv,
    couple_low,
    couple_up,
    sep_lower_inv,
    sep_upper_inv,
    basis_sub,
    basis_sep,
):
    vec_count, row_count = rhs_sub.shape
    border = couple_low.shape[0]
    high = lax.Precision.HIGHEST
    live_mask = lax.broadcasted_iota(jnp.int32, (1, row_count), 1) < live_rows[0]
    lower_sol = jnp.where(live_mask, apply_blocks(rhs_sub, lower_inv), 0.0)
    border_rows = lower_sol[:, :border].astype(jnp.bfloat16)
    columns = couple_low
    top_block = lax.psum_scatter(
        lax.dot_general(
            columns, border_rows, (((0,), (1,)), ((), ())), preferred_element_type=jnp.float32
        ),
        "leaf",
        scatter_dimension=0,
        tiled=True,
    )
    top_block = lax.psum(top_block, "front")
    top_rhs = rhs_sep - top_block.T
    lower_part = jnp.dot(
        top_rhs.astype(jnp.bfloat16), sep_lower_inv, preferred_element_type=jnp.float32
    )
    top_lower = lax.psum(lower_part, "leaf")
    upper_part = lax.dot_general(
        top_lower.astype(jnp.bfloat16),
        sep_upper_inv,
        (((1,), (1,)), ((), ())),
        preferred_element_type=jnp.float32,
    )
    top_sol = lax.psum(upper_part, "front")
    columns = couple_up
    correction = lax.dot_general(
        lax.all_gather(top_sol.astype(jnp.bfloat16), "leaf", axis=1, tiled=True),
        columns,
        (((1,), (1,)), ((), ())),
        preferred_element_type=jnp.float32,
    )
    updated = jnp.concatenate([lower_sol[:, :border] - correction, lower_sol[:, border:]], axis=1)
    upper_sol = jnp.where(live_mask, apply_blocks(updated, upper_inv), 0.0)
    coef_sum = jnp.zeros((basis_sub.shape[0], vec_count), jnp.float32)
    for sweep in range(2):
        local_sub = lax.dot_general(basis_sub, upper_sol, (((1,), (1,)), ((), ())), precision=high)
        local_sep = lax.dot_general(basis_sep, top_sol, (((1,), (1,)), ((), ())), precision=high)
        coef_pass = lax.psum(local_sub, ("leaf", "front")) + lax.psum(local_sep, "leaf")
        part_sub = upper_sol
        part_sep = top_sol
        part_sub = part_sub - lax.dot_general(
            coef_pass, basis_sub, (((0,), (0,)), ((), ())), precision=high
        )
        part_sep = part_sep - lax.dot_general(
            coef_pass, basis_sep, (((0,), (0,)), ((), ())), precision=high
        )
        upper_sol = part_sub
        top_sol = part_sep
        coef_sum = coef_sum + coef_pass
    return (upper_sol, top_sol, coef_sum)


def solution(mesh):
    leaves, fronts = mesh.shape["leaf"], mesh.shape["front"]

    def local(*arrays):
        piece = arrays[1].shape[1] // fronts
        paired = leaves > 2 and fronts > 2 and not (leaves & (leaves - 1) or fronts & (fronts - 1))
        if paired and piece % 256 == 0 and arrays[0].shape[0] == 8:
            return fused_shards(leaves, fronts, *arrays)
        return shards(*arrays)

    return jax.shard_map(
        local,
        mesh=mesh,
        in_specs=(
            P(None, ("leaf", "front")),
            P(None, "leaf"),
            P(("leaf", "front")),
            P(("leaf", "front"), None, None),
            P(("leaf", "front"), None, None),
            P(("leaf", "front"), None),
            P(("leaf", "front"), None),
            P("leaf", "front"),
            P("leaf", "front"),
            P(None, ("leaf", "front")),
            P(None, "leaf"),
        ),
        out_specs=(P(None, ("leaf", "front")), P(None, "leaf"), P()),
        check_vma=False,
    )
```

```python
import functools

import jax
import jax.numpy as jnp
from jax import lax
from jax.experimental import pallas as pl
from jax.experimental.pallas import tpu as pltpu
from jax.sharding import PartitionSpec as P

MESH = pl.DeviceIdType.MESH
HIGH = lax.Precision.HIGHEST
LAST = (((1,), (1,)), ((), ()))
A_PAIR, A_SUM, A_ALL, B_SUM, B_ALL, C_SUM, S_ALL = range(7)
D_ALL, D_PAIR, G_FRONT, G_LEAF, H_FRONT, H_LEAF = range(7, 13)


def fold(piece):
    half = piece.shape[1] // 2
    return jnp.concatenate([piece[:, :half], piece[:, half:]], axis=0)


def unfold(piece):
    piece = piece.astype(jnp.float32)
    rows = piece.shape[0] // 2
    return jnp.concatenate([piece[:rows], piece[rows:]], axis=1)


def exact(left, right, dims=LAST):
    return lax.dot_general(left, right, dims, precision=HIGH, preferred_element_type=jnp.float32)


def flip(index, k):
    bit, result = 1, index
    while bit <= k:
        if k & bit:
            result = result + bit * (1 - 2 * lax.rem(index // bit, 2))
        bit *= 2
    return result


def hand_over(*refs):
    given, placed, held, (into, out) = refs[:3], refs[3:6], refs[6:9], refs[9:]
    reads = [pltpu.make_async_copy(given[k], held[k], into.at[k]) for k in range(3)]
    writes = [pltpu.make_async_copy(held[k], placed[k], out.at[k]) for k in range(3)]
    for copy in reads:
        copy.start()
    for read, write in zip(reads, writes):
        read.wait()
        write.start()
    for copy in writes:
        copy.wait()


def fused(
    leaves,
    fronts,
    live_rows,
    rhs_sub,
    rhs_sep,
    lower_inv,
    upper_inv,
    couple_low,
    couple_up,
    sep_lower,
    sep_upper,
    basis_sub,
    basis_sep,
    orth_sub,
    orth_sep,
    coef,
    rhs_sub_v,
    rhs_sep_v,
    lower_v,
    upper_v,
    clow_v,
    cup_v,
    slow_v,
    sup_v,
    bsub_v,
    bsep_v,
    low_v,
    sol_v,
    a_part,
    a_pair,
    a_send,
    a_recv,
    t_buf,
    b_acc,
    b_send,
    b_recv,
    l_buf,
    c_acc,
    c_send,
    c_recv,
    s_buf,
    d_buf,
    g_front,
    g_leaf,
    h_front,
    h_leaf,
    load,
    send,
    recv,
    recv_pair,
    recv_front,
    recv_leaf,
    live,
):
    leaf, front = lax.axis_index("leaf"), lax.axis_index("front")
    half, per_leaf = leaves * fronts // 2, fronts // 2
    parity, place = lax.rem(front, 2), leaf * per_leaf + front // 2
    mate = (leaf, flip(front, 1))
    blocks, size, _ = lower_v.shape
    border = clow_v.shape[0]
    width = s_buf.shape[2]
    basis = bsub_v.shape[0]

    def fetch(source, target, slot):
        return pltpu.make_async_copy(source, target, load.at[slot])

    def push(source, target, step, device, arrived=None):
        pltpu.make_async_remote_copy(
            src_ref=source,
            dst_ref=target,
            send_sem=send.at[step],
            recv_sem=recv.at[step] if arrived is None else arrived,
            device_id=device,
            device_id_type=MESH,
        ).start()

    def drain(view, sem):
        pltpu.make_async_copy(view, view, sem).wait()

    def device(k):
        return flip(leaf, k // per_leaf), flip(front, 2 * (k % per_leaf))

    def columns(index):
        return pl.ds(pl.multiple_of(index * width, width), width)

    first = [
        fetch(rhs_sub, rhs_sub_v, 0),
        fetch(lower_inv.at[pl.ds(0, 1)], lower_v.at[pl.ds(0, 1)], 1),
        fetch(couple_low, clow_v, 2),
        fetch(live_rows, live, 11),
    ]
    second = [
        fetch(rhs_sep, rhs_sep_v, 3),
        fetch(lower_inv.at[pl.ds(1, blocks - 1)], lower_v.at[pl.ds(1, blocks - 1)], 4),
        fetch(upper_inv, upper_v, 5),
        fetch(basis_sub, bsub_v, 6),
        fetch(basis_sep, bsep_v, 7),
    ]

    def fetch_rows(source, target, slot):
        rows = source.shape[0] // 4
        for k in range(4):
            some = pl.ds(k * rows, rows)
            fetch(source.at[some], target.at[some], slot).start()

    for copy in first:
        copy.start()

    barrier = pltpu.get_barrier_semaphore()

    for k in range(1, half):
        pl.semaphore_signal(barrier, inc=1, device_id=device(k), device_id_type=MESH)
    for k in range(1, fronts, 2):
        pl.semaphore_signal(
            barrier, inc=1, device_id=(leaf, flip(front, k)), device_id_type=MESH
        )
    for copy in second:
        copy.start()

    def live_part(value, k):
        row = lax.broadcasted_iota(jnp.int32, value.shape, 1) + k * size
        return jnp.where(row < live[0], value, 0.0)

    def lower_block(k):
        part = rhs_sub_v[:, k * size : (k + 1) * size].astype(jnp.bfloat16)
        return live_part(jnp.dot(part, lower_v[k], preferred_element_type=jnp.float32), k)

    def upper_block(value, k):
        part = value.astype(jnp.bfloat16)
        return live_part(jnp.dot(part, upper_v[k], preferred_element_type=jnp.float32), k)

    first[0].wait()
    first[1].wait()
    first[3].wait()
    low_v[...] = lower_block(0)
    border_rows = low_v[:, :border].astype(jnp.bfloat16)
    first[2].wait()
    fetch_rows(sep_lower, slow_v, 8)

    greeted = False
    for group in range(2):
        ahead, some = group * (half // 2), half // 2
        for q in range(ahead, ahead + some):
            for p in range(2):
                at = (2 * q + p) * width
                a_part[p, q] = jnp.dot(
                    border_rows, clow_v[:, at : at + width], preferred_element_type=jnp.float32
                )
        if not greeted:
            pl.semaphore_wait(barrier, half - 1 + fronts // 2)
            greeted = True
        push(
            a_part.at[1 - parity, pl.ds(ahead, some)],
            a_pair.at[pl.ds(ahead, some)],
            A_PAIR,
            mate,
            recv_pair.at[group],
        )
    second[0].wait()
    for group in range(2):
        ahead, some = group * (half // 2), half // 2
        drain(a_pair.at[pl.ds(ahead, some)], recv_pair.at[group])
        for q in range(ahead, ahead + some):
            a_send[q] = fold(a_part[parity, q] + a_pair[q]).astype(jnp.bfloat16)

    for k in range(half - 1, 0, -1):
        push(a_send.at[flip(place, k)], a_recv.at[k - 1], A_SUM, device(k))

    second[3].wait()
    second[4].wait()
    own = bsep_v[:, columns(front)]
    gram = exact(bsub_v[...], bsub_v[...]) + exact(own, own)
    g_front[front] = jnp.zeros(g_front.shape[1:], jnp.float32)
    g_front[front, :, 0:basis] = gram
    for k in range(1, fronts):
        push(g_front.at[front], g_front.at[front], G_FRONT, (leaf, flip(front, k)))
    top = rhs_sep_v[:, columns(front)] - (a_part[parity, place] + a_pair[place])

    drain(a_recv, recv.at[A_SUM])
    top = fold(top) - jnp.sum(a_recv[...].astype(jnp.float32), axis=0)
    t_buf[0] = top.astype(jnp.bfloat16)
    for k in range(fronts - 1, 0, -1):
        push(t_buf.at[0], t_buf.at[k], A_ALL, (leaf, flip(front, k)), recv_front.at[k])

    def strip(index):
        return pl.ds(pl.multiple_of(index * width, width), width)

    def top_piece(k):
        if k:
            drain(t_buf.at[k], recv_front.at[k])
        return unfold(t_buf[k]).astype(jnp.bfloat16), strip(flip(front, k))

    def times_lower(piece, to):
        return jnp.dot(piece[0], slow_v[piece[1], to], preferred_element_type=jnp.float32)

    drain(slow_v, load.at[8])
    fetch_rows(sep_upper, sup_v, 9)
    fetch(couple_up, cup_v, 10).start()
    for k in range(fronts - 2):
        piece = top_piece(k)
        for n in range(leaves):
            product = times_lower(piece, slice(n * width, (n + 1) * width))
            b_acc[n] = b_acc[n] + product if k else product
        if k == 0:
            drain(g_front.at[pl.ds(0, fronts - 1)], recv.at[G_FRONT])
            g_leaf[leaf] = jnp.sum(g_front[...], axis=0)
            for j in range(1, leaves):
                push(g_leaf.at[leaf], g_leaf.at[leaf], G_LEAF, (flip(leaf, j), front))
    last = [top_piece(k) for k in range(fronts - 2, fronts)]

    def lower_piece(to):
        return b_acc[to] + sum(times_lower(piece, columns(to)) for piece in last)

    for k in range(leaves - 1, 0, -1):
        to = flip(leaf, k)
        b_send[k - 1] = lower_piece(to)
        push(b_send.at[k - 1], b_recv.at[k - 1], B_SUM, (to, front))
    piece = lower_piece(leaf)
    drain(b_recv, recv.at[B_SUM])
    piece = piece + jnp.sum(b_recv[...], axis=0)
    l_buf[0] = fold(piece).astype(jnp.bfloat16)
    for k in range(leaves - 1, 0, -1):
        push(l_buf.at[0], l_buf.at[k], B_ALL, (flip(leaf, k), front), recv_leaf.at[k])

    def low_piece(k):
        if k:
            drain(l_buf.at[k], recv_leaf.at[k])
        return unfold(l_buf[k]).astype(jnp.bfloat16), columns(flip(leaf, k))

    def times_upper(piece, to):
        return lax.dot_general(
            sup_v[to, piece[1]], piece[0], LAST, preferred_element_type=jnp.float32
        )

    drain(sup_v, load.at[9])
    for group in (range(0, 1), range(1, 2), range(2, leaves // 2)):
        pieces = [low_piece(k) for k in group]
        if not pieces:
            continue
        for n in range(fronts):
            to = slice(n * width, (n + 1) * width)
            product = sum(times_upper(piece, to) for piece in pieces)
            c_acc[n] = c_acc[n] + product if group[0] else product
    last2 = [low_piece(k) for k in range(max(2, leaves // 2), leaves)]

    def upper_piece(to):
        return jnp.transpose(
            c_acc[to] + sum(times_upper(piece, strip(to)) for piece in last2)
        )

    for k in range(fronts - 1, 0, -1):
        to = flip(front, k)
        c_send[k - 1] = upper_piece(to)
        push(c_send.at[k - 1], c_recv.at[k - 1], C_SUM, (leaf, to))
    piece = upper_piece(front)
    drain(c_recv, recv.at[C_SUM])
    piece = piece + jnp.sum(c_recv[...], axis=0)

    d_buf[parity, place] = fold(piece).astype(jnp.bfloat16)
    mine = d_buf.at[parity, place]

    for k in range(half - 1, 0, -1):
        push(mine, mine, D_ALL, device(k))
    s_buf[front] = piece
    for k in range(1, fronts):
        push(s_buf.at[front], s_buf.at[front], S_ALL, (leaf, flip(front, k)))

    second[1].wait()
    second[2].wait()
    for k in range(1, blocks):
        sol_v[:, k * size : (k + 1) * size] = upper_block(lower_block(k), k)
    early = exact(sol_v[:, size:], bsub_v[:, size:]) + exact(piece, bsep_v[:, columns(front)])
    drain(cup_v, load.at[10])

    def correct(p):
        return sum(
            lax.dot_general(
                unfold(d_buf[p, q]).astype(jnp.bfloat16),
                cup_v[:, columns(2 * q + p)],
                LAST,
                preferred_element_type=jnp.float32,
            )
            for q in range(half)
        )

    drain(d_buf.at[0, pl.ds(0, half - 1)], recv.at[D_ALL])
    push(d_buf.at[parity], d_buf.at[parity], D_PAIR, mate)
    correction = correct(parity)
    drain(d_buf.at[0], recv.at[D_PAIR])
    correction = correction + correct(1 - parity)
    low_v[:, 0:border] = low_v[:, 0:border] - correction
    sol_v[:, 0:size] = upper_block(low_v[...], 0)
    h_front[front] = jnp.zeros(h_front.shape[1:], jnp.float32)
    h_front[front, :, 0:basis] = early + exact(sol_v[:, 0:size], bsub_v[:, 0:size])
    for k in range(fronts - 1, 0, -1):
        push(h_front.at[front], h_front.at[front], H_FRONT, (leaf, flip(front, k)))
    drain(g_leaf.at[pl.ds(0, leaves - 1)], recv.at[G_LEAF])
    gram = jnp.sum(g_leaf[...], axis=0)[:, 0:basis]
    drain(h_front.at[pl.ds(0, fronts - 1)], recv.at[H_FRONT])
    h_leaf[leaf] = jnp.sum(h_front[...], axis=0)
    for k in range(leaves - 1, 0, -1):
        push(h_leaf.at[leaf], h_leaf.at[leaf], H_LEAF, (flip(leaf, k), front))
    drain(s_buf.at[pl.ds(0, fronts - 1)], recv.at[S_ALL])
    rows_cols = (((1,), (0,)), ((), ()))
    twice = 2.0 * (
        lax.broadcasted_iota(jnp.int32, gram.shape, 0)
        == lax.broadcasted_iota(jnp.int32, gram.shape, 1)
    ).astype(jnp.float32) - gram
    bsub_v[...] = exact(twice, bsub_v[...], rows_cols)
    bsep_v[...] = exact(twice, bsep_v[...], rows_cols)
    drain(h_leaf.at[pl.ds(0, leaves - 1)], recv.at[H_LEAF])

    once = jnp.sum(h_leaf[...], axis=0)[:, 0:basis]
    orth_sub[...] = sol_v[...] - exact(once, bsub_v[...], rows_cols)
    top_sol = jnp.concatenate([s_buf[k] for k in range(fronts)], axis=1)
    orth_sep[...] = top_sol - exact(once, bsep_v[...], rows_cols)
    coef[...] = once + (once - exact(once, gram, rows_cols))

    drain(a_pair, send.at[A_PAIR])
    drain(a_recv, send.at[A_SUM])
    drain(t_buf.at[pl.ds(0, fronts - 1)], send.at[A_ALL])
    drain(b_recv, send.at[B_SUM])
    drain(l_buf.at[pl.ds(0, leaves - 1)], send.at[B_ALL])
    drain(c_recv, send.at[C_SUM])
    drain(s_buf.at[pl.ds(0, fronts - 1)], send.at[S_ALL])
    drain(d_buf.at[0, pl.ds(0, half - 1)], send.at[D_ALL])
    drain(d_buf.at[0], send.at[D_PAIR])
    drain(g_front.at[pl.ds(0, fronts - 1)], send.at[G_FRONT])
    drain(g_leaf.at[pl.ds(0, leaves - 1)], send.at[G_LEAF])
    drain(h_front.at[pl.ds(0, fronts - 1)], send.at[H_FRONT])
    drain(h_leaf.at[pl.ds(0, leaves - 1)], send.at[H_LEAF])


def fused_shards(
    leaves,
    fronts,
    rhs_sub,
    rhs_sep,
    live_rows,
    lower_inv,
    upper_inv,
    couple_low,
    couple_up,
    sep_lower_inv,
    sep_upper_inv,
    basis_sub,
    basis_sep,
):
    vecs, basis = rhs_sub.shape[0], basis_sub.shape[0]
    half = leaves * fronts // 2
    width = rhs_sep.shape[1] // fronts
    size = lower_inv.shape[1]
    full = [
        rhs_sub, rhs_sep, lower_inv, upper_inv, couple_low, couple_up,
        sep_lower_inv, sep_upper_inv, basis_sub, basis_sep,
    ]
    lanes = -(-basis // 128) * 128
    narrow = (2 * vecs, width // 2)

    def wide(*shape):
        return pltpu.VMEM(shape, jnp.float32)

    def slim(slots):
        return pltpu.VMEM((slots,) + narrow, jnp.bfloat16)

    vmem = pl.BlockSpec(memory_space=pltpu.VMEM)
    anywhere = pl.BlockSpec(memory_space=pltpu.HBM)
    parts = pl.pallas_call(
        functools.partial(fused, leaves, fronts),
        out_shape=(
            jax.ShapeDtypeStruct(rhs_sub.shape, jnp.float32),
            jax.ShapeDtypeStruct(rhs_sep.shape, jnp.float32),
            jax.ShapeDtypeStruct((vecs, basis), jnp.float32),
        ),
        in_specs=[anywhere] * (len(full) + 1),
        out_specs=(vmem, vmem, vmem),
        scratch_shapes=[pltpu.VMEM(x.shape, x.dtype) for x in full]
        + [
            wide(vecs, size),
            wide(*rhs_sub.shape),
            wide(2, half, vecs, width),
            wide(half, vecs, width),
            slim(half),
            slim(half - 1),
            slim(fronts),
            wide(leaves, vecs, width),
            wide(leaves - 1, vecs, width),
            wide(leaves - 1, vecs, width),
            slim(leaves),
            wide(fronts, width, vecs),
            wide(fronts - 1, vecs, width),
            wide(fronts - 1, vecs, width),
            wide(fronts, vecs, width),
            pltpu.VMEM((2, half) + narrow, jnp.bfloat16),
            wide(fronts, basis, lanes),
            wide(leaves, basis, lanes),
            wide(fronts, vecs, lanes),
            wide(leaves, vecs, lanes),
            pltpu.SemaphoreType.DMA((12,)),
            pltpu.SemaphoreType.DMA((13,)),
            pltpu.SemaphoreType.DMA((13,)),
            pltpu.SemaphoreType.DMA((2,)),
            pltpu.SemaphoreType.DMA((fronts,)),
            pltpu.SemaphoreType.DMA((leaves,)),
            pltpu.SMEM(live_rows.shape, jnp.int32),
        ],
        compiler_params=pltpu.CompilerParams(
            collective_id=0, has_side_effects=True, vmem_limit_bytes=56 * 1024 * 1024
        ),
    )(live_rows, *full)
    orth_sub, orth_sep, coef = pl.pallas_call(
        hand_over,
        out_shape=tuple(jax.ShapeDtypeStruct(x.shape, x.dtype) for x in parts),
        in_specs=[anywhere] * 3,
        out_specs=(anywhere,) * 3,
        scratch_shapes=[pltpu.VMEM(x.shape, x.dtype) for x in parts]
        + [pltpu.SemaphoreType.DMA((3,))] * 2,
        compiler_params=pltpu.CompilerParams(vmem_limit_bytes=56 * 1024 * 1024),
    )(*parts)
    return orth_sub, orth_sep, coef.T


def apply_blocks(vectors, inverse):
    vec_count = vectors.shape[0]
    shaped = vectors.astype(jnp.bfloat16).reshape(vec_count, inverse.shape[0], inverse.shape[1])
    product = jnp.einsum("vkr,krc->vkc", shaped, inverse, preferred_element_type=jnp.float32)
    return product.reshape(vec_count, inverse.shape[0] * inverse.shape[2])


def shards(
    rhs_sub,
    rhs_sep,
    live_rows,
    lower_inv,
    upper_inv,
    couple_low,
    couple_up,
    sep_lower_inv,
    sep_upper_inv,
    basis_sub,
    basis_sep,
):
    vec_count, row_count = rhs_sub.shape
    border = couple_low.shape[0]
    high = lax.Precision.HIGHEST
    live_mask = lax.broadcasted_iota(jnp.int32, (1, row_count), 1) < live_rows[0]
    lower_sol = jnp.where(live_mask, apply_blocks(rhs_sub, lower_inv), 0.0)
    border_rows = lower_sol[:, :border].astype(jnp.bfloat16)
    columns = couple_low
    top_block = lax.psum_scatter(
        lax.dot_general(
            columns, border_rows, (((0,), (1,)), ((), ())), preferred_element_type=jnp.float32
        ),
        "leaf",
        scatter_dimension=0,
        tiled=True,
    )
    top_block = lax.psum(top_block, "front")
    top_rhs = rhs_sep - top_block.T
    lower_part = jnp.dot(
        top_rhs.astype(jnp.bfloat16), sep_lower_inv, preferred_element_type=jnp.float32
    )
    top_lower = lax.psum(lower_part, "leaf")
    upper_part = lax.dot_general(
        top_lower.astype(jnp.bfloat16),
        sep_upper_inv,
        (((1,), (1,)), ((), ())),
        preferred_element_type=jnp.float32,
    )
    top_sol = lax.psum(upper_part, "front")
    columns = couple_up
    correction = lax.dot_general(
        lax.all_gather(top_sol.astype(jnp.bfloat16), "leaf", axis=1, tiled=True),
        columns,
        (((1,), (1,)), ((), ())),
        preferred_element_type=jnp.float32,
    )
    updated = jnp.concatenate([lower_sol[:, :border] - correction, lower_sol[:, border:]], axis=1)
    upper_sol = jnp.where(live_mask, apply_blocks(updated, upper_inv), 0.0)
    coef_sum = jnp.zeros((basis_sub.shape[0], vec_count), jnp.float32)
    for sweep in range(2):
        local_sub = lax.dot_general(basis_sub, upper_sol, (((1,), (1,)), ((), ())), precision=high)
        local_sep = lax.dot_general(basis_sep, top_sol, (((1,), (1,)), ((), ())), precision=high)
        coef_pass = lax.psum(local_sub, ("leaf", "front")) + lax.psum(local_sep, "leaf")
        part_sub = upper_sol
        part_sep = top_sol
        part_sub = part_sub - lax.dot_general(
            coef_pass, basis_sub, (((0,), (0,)), ((), ())), precision=high
        )
        part_sep = part_sep - lax.dot_general(
            coef_pass, basis_sep, (((0,), (0,)), ((), ())), precision=high
        )
        upper_sol = part_sub
        top_sol = part_sep
        coef_sum = coef_sum + coef_pass
    return (upper_sol, top_sol, coef_sum)


def solution(mesh):
    leaves, fronts = mesh.shape["leaf"], mesh.shape["front"]

    def local(*arrays):
        piece = arrays[1].shape[1] // fronts
        paired = leaves > 2 and fronts > 2 and not (leaves & (leaves - 1) or fronts & (fronts - 1))
        if paired and piece % 256 == 0 and arrays[0].shape[0] == 8:
            return fused_shards(leaves, fronts, *arrays)
        return shards(*arrays)

    return jax.shard_map(
        local,
        mesh=mesh,
        in_specs=(
            P(None, ("leaf", "front")),
            P(None, "leaf"),
            P(("leaf", "front")),
            P(("leaf", "front"), None, None),
            P(("leaf", "front"), None, None),
            P(("leaf", "front"), None),
            P(("leaf", "front"), None),
            P("leaf", "front"),
            P("leaf", "front"),
            P(None, ("leaf", "front")),
            P(None, "leaf"),
        ),
        out_specs=(P(None, ("leaf", "front")), P(None, "leaf"), P()),
        check_vma=False,
    )
```

```python
import functools

import jax
import jax.numpy as jnp
from jax import lax
from jax.experimental import pallas as pl
from jax.experimental.pallas import tpu as pltpu
from jax.sharding import PartitionSpec as P

MESH = pl.DeviceIdType.MESH
HIGH = lax.Precision.HIGHEST
LAST = (((1,), (1,)), ((), ()))
A_PAIR, A_SUM, A_ALL, B_SUM, B_ALL, C_SUM, S_ALL = range(7)
D_ALL, D_PAIR, G_FRONT, G_LEAF, H_FRONT, H_LEAF = range(7, 13)


def fold(piece):
    half = piece.shape[1] // 2
    return jnp.concatenate([piece[:, :half], piece[:, half:]], axis=0)


def unfold(piece):
    piece = piece.astype(jnp.float32)
    rows = piece.shape[0] // 2
    return jnp.concatenate([piece[:rows], piece[rows:]], axis=1)


def exact(left, right, dims=LAST):
    return lax.dot_general(left, right, dims, precision=HIGH, preferred_element_type=jnp.float32)


def flip(index, k):
    bit, result = 1, index
    while bit <= k:
        if k & bit:
            result = result + bit * (1 - 2 * lax.rem(index // bit, 2))
        bit *= 2
    return result


def hand_over(*refs):
    given, placed, held, (into, out) = refs[:3], refs[3:6], refs[6:9], refs[9:]
    reads = [pltpu.make_async_copy(given[k], held[k], into.at[k]) for k in range(3)]
    writes = [pltpu.make_async_copy(held[k], placed[k], out.at[k]) for k in range(3)]
    for copy in reads:
        copy.start()
    for read, write in zip(reads, writes):
        read.wait()
        write.start()
    for copy in writes:
        copy.wait()


def fused(
    leaves,
    fronts,
    live_rows,
    rhs_sub,
    rhs_sep,
    lower_inv,
    upper_inv,
    couple_low,
    couple_up,
    sep_lower,
    sep_upper,
    basis_sub,
    basis_sep,
    orth_sub,
    orth_sep,
    coef,
    rhs_sub_v,
    rhs_sep_v,
    lower_v,
    upper_v,
    clow_v,
    cup_v,
    slow_v,
    sup_v,
    bsub_v,
    bsep_v,
    low_v,
    sol_v,
    a_part,
    a_pair,
    a_send,
    a_recv,
    t_buf,
    b_acc,
    b_send,
    b_recv,
    l_buf,
    c_acc,
    c_send,
    c_recv,
    s_buf,
    d_buf,
    g_front,
    g_leaf,
    h_front,
    h_leaf,
    load,
    send,
    recv,
    recv_pair,
    recv_front,
    recv_leaf,
    live,
):
    leaf, front = lax.axis_index("leaf"), lax.axis_index("front")
    half, per_leaf = leaves * fronts // 2, fronts // 2
    parity, place = lax.rem(front, 2), leaf * per_leaf + front // 2
    mate = (leaf, flip(front, 1))
    blocks, size, _ = lower_v.shape
    border = clow_v.shape[0]
    width = s_buf.shape[2]
    basis = bsub_v.shape[0]

    def fetch(source, target, slot):
        return pltpu.make_async_copy(source, target, load.at[slot])

    def push(source, target, step, device, arrived=None):
        pltpu.make_async_remote_copy(
            src_ref=source,
            dst_ref=target,
            send_sem=send.at[step],
            recv_sem=recv.at[step] if arrived is None else arrived,
            device_id=device,
            device_id_type=MESH,
        ).start()

    def drain(view, sem):
        pltpu.make_async_copy(view, view, sem).wait()

    def device(k):
        return flip(leaf, k // per_leaf), flip(front, 2 * (k % per_leaf))

    def columns(index):
        return pl.ds(pl.multiple_of(index * width, width), width)

    first = [
        fetch(rhs_sub, rhs_sub_v, 0),
        fetch(lower_inv.at[pl.ds(0, 1)], lower_v.at[pl.ds(0, 1)], 1),
        fetch(couple_low, clow_v, 2),
        fetch(live_rows, live, 11),
    ]
    second = [
        fetch(rhs_sep, rhs_sep_v, 3),
        fetch(lower_inv.at[pl.ds(1, blocks - 1)], lower_v.at[pl.ds(1, blocks - 1)], 4),
        fetch(upper_inv, upper_v, 5),
        fetch(basis_sub, bsub_v, 6),
        fetch(basis_sep, bsep_v, 7),
    ]

    def fetch_rows(source, target, slot):
        rows = source.shape[0] // 4
        for k in range(4):
            some = pl.ds(k * rows, rows)
            fetch(source.at[some], target.at[some], slot).start()

    for copy in first:
        copy.start()

    barrier = pltpu.get_barrier_semaphore()

    for k in range(1, half):
        pl.semaphore_signal(barrier, inc=1, device_id=device(k), device_id_type=MESH)
    for k in range(1, fronts, 2):
        pl.semaphore_signal(
            barrier, inc=1, device_id=(leaf, flip(front, k)), device_id_type=MESH
        )
    for copy in second:
        copy.start()

    def live_part(value, k):
        row = lax.broadcasted_iota(jnp.int32, value.shape, 1) + k * size
        return jnp.where(row < live[0], value, 0.0)

    def lower_block(k):
        part = rhs_sub_v[:, k * size : (k + 1) * size].astype(jnp.bfloat16)
        return live_part(jnp.dot(part, lower_v[k], preferred_element_type=jnp.float32), k)

    def upper_block(value, k):
        part = value.astype(jnp.bfloat16)
        return live_part(jnp.dot(part, upper_v[k], preferred_element_type=jnp.float32), k)

    first[0].wait()
    first[1].wait()
    first[3].wait()
    low_v[...] = lower_block(0)
    border_rows = low_v[:, :border].astype(jnp.bfloat16)
    first[2].wait()
    fetch_rows(sep_lower, slow_v, 8)

    greeted = False
    for group in range(2):
        ahead, some = group * (half // 2), half // 2
        for q in range(ahead, ahead + some):
            for p in range(2):
                at = (2 * q + p) * width
                a_part[p, q] = jnp.dot(
                    border_rows, clow_v[:, at : at + width], preferred_element_type=jnp.float32
                )
        if not greeted:
            pl.semaphore_wait(barrier, half - 1 + fronts // 2)
            greeted = True
        push(
            a_part.at[1 - parity, pl.ds(ahead, some)],
            a_pair.at[pl.ds(ahead, some)],
            A_PAIR,
            mate,
            recv_pair.at[group],
        )
    second[0].wait()
    for group in range(2):
        ahead, some = group * (half // 2), half // 2
        drain(a_pair.at[pl.ds(ahead, some)], recv_pair.at[group])
        for q in range(ahead, ahead + some):
            a_send[q] = fold(a_part[parity, q] + a_pair[q]).astype(jnp.bfloat16)

    for k in range(half - 1, 0, -1):
        push(a_send.at[flip(place, k)], a_recv.at[k - 1], A_SUM, device(k))

    second[3].wait()
    second[4].wait()
    own = bsep_v[:, columns(front)]
    gram = exact(bsub_v[...], bsub_v[...]) + exact(own, own)
    g_front[front] = jnp.zeros(g_front.shape[1:], jnp.float32)
    g_front[front, :, 0:basis] = gram
    for k in range(1, fronts):
        push(g_front.at[front], g_front.at[front], G_FRONT, (leaf, flip(front, k)))
    top = rhs_sep_v[:, columns(front)] - (a_part[parity, place] + a_pair[place])

    drain(a_recv, recv.at[A_SUM])
    top = fold(top) - jnp.sum(a_recv[...].astype(jnp.float32), axis=0)
    t_buf[0] = top.astype(jnp.bfloat16)
    for k in range(fronts - 1, 0, -1):
        push(t_buf.at[0], t_buf.at[k], A_ALL, (leaf, flip(front, k)), recv_front.at[k])

    def strip(index):
        return pl.ds(pl.multiple_of(index * width, width), width)

    def top_piece(k):
        if k:
            drain(t_buf.at[k], recv_front.at[k])
        return unfold(t_buf[k]).astype(jnp.bfloat16), strip(flip(front, k))

    def times_lower(piece, to):
        return jnp.dot(piece[0], slow_v[piece[1], to], preferred_element_type=jnp.float32)

    drain(slow_v, load.at[8])
    fetch_rows(sep_upper, sup_v, 9)
    fetch(couple_up, cup_v, 10).start()
    for k in range(fronts - 2):
        piece = top_piece(k)
        for n in range(leaves):
            product = times_lower(piece, slice(n * width, (n + 1) * width))
            b_acc[n] = b_acc[n] + product if k else product
    last = [top_piece(k) for k in range(fronts - 2, fronts)]

    def lower_piece(to):
        return b_acc[to] + sum(times_lower(piece, columns(to)) for piece in last)

    for k in range(leaves - 1, 0, -1):
        to = flip(leaf, k)
        b_send[k - 1] = fold(lower_piece(to)).astype(jnp.bfloat16)
        push(b_send.at[k - 1], b_recv.at[k - 1], B_SUM, (to, front))
    piece = lower_piece(leaf)
    drain(b_recv, recv.at[B_SUM])
    piece = fold(piece) + jnp.sum(b_recv[...].astype(jnp.float32), axis=0)
    l_buf[0] = piece.astype(jnp.bfloat16)
    for k in range(leaves - 1, 0, -1):
        push(l_buf.at[0], l_buf.at[k], B_ALL, (flip(leaf, k), front), recv_leaf.at[k])

    def low_piece(k):
        if k:
            drain(l_buf.at[k], recv_leaf.at[k])
        return unfold(l_buf[k]).astype(jnp.bfloat16), columns(flip(leaf, k))

    def times_upper(piece, to):
        return lax.dot_general(
            sup_v[to, piece[1]], piece[0], LAST, preferred_element_type=jnp.float32
        )

    drain(sup_v, load.at[9])
    for group in (range(0, 1), range(1, 2), range(2, leaves // 2)):
        pieces = [low_piece(k) for k in group]
        if not pieces:
            continue
        for n in range(fronts):
            to = slice(n * width, (n + 1) * width)
            product = sum(times_upper(piece, to) for piece in pieces)
            c_acc[n] = c_acc[n] + product if group[0] else product
    last2 = [low_piece(k) for k in range(max(2, leaves // 2), leaves)]
    drain(g_front.at[pl.ds(0, fronts - 1)], recv.at[G_FRONT])
    g_leaf[leaf] = jnp.sum(g_front[...], axis=0)
    for k in range(1, leaves):
        push(g_leaf.at[leaf], g_leaf.at[leaf], G_LEAF, (flip(leaf, k), front))

    def upper_piece(to):
        return jnp.transpose(
            c_acc[to] + sum(times_upper(piece, strip(to)) for piece in last2)
        )

    for k in range(fronts - 1, 0, -1):
        to = flip(front, k)
        c_send[k - 1] = upper_piece(to)
        push(c_send.at[k - 1], c_recv.at[k - 1], C_SUM, (leaf, to))
    piece = upper_piece(front)
    drain(c_recv, recv.at[C_SUM])
    piece = piece + jnp.sum(c_recv[...], axis=0)

    d_buf[parity, place] = fold(piece).astype(jnp.bfloat16)
    mine = d_buf.at[parity, place]

    for k in range(half - 1, 0, -1):
        push(mine, mine, D_ALL, device(k))
    s_buf[front] = piece
    for k in range(1, fronts):
        push(s_buf.at[front], s_buf.at[front], S_ALL, (leaf, flip(front, k)))

    second[1].wait()
    second[2].wait()
    for k in range(1, blocks):
        sol_v[:, k * size : (k + 1) * size] = upper_block(lower_block(k), k)
    early = exact(sol_v[:, size:], bsub_v[:, size:]) + exact(piece, bsep_v[:, columns(front)])
    drain(cup_v, load.at[10])

    def correct(p):
        return sum(
            lax.dot_general(
                unfold(d_buf[p, q]).astype(jnp.bfloat16),
                cup_v[:, columns(2 * q + p)],
                LAST,
                preferred_element_type=jnp.float32,
            )
            for q in range(half)
        )

    drain(d_buf.at[0, pl.ds(0, half - 1)], recv.at[D_ALL])
    push(d_buf.at[parity], d_buf.at[parity], D_PAIR, mate)
    correction = correct(parity)
    drain(d_buf.at[0], recv.at[D_PAIR])
    correction = correction + correct(1 - parity)
    low_v[:, 0:border] = low_v[:, 0:border] - correction
    sol_v[:, 0:size] = upper_block(low_v[...], 0)
    h_front[front] = jnp.zeros(h_front.shape[1:], jnp.float32)
    h_front[front, :, 0:basis] = early + exact(sol_v[:, 0:size], bsub_v[:, 0:size])
    for k in range(fronts - 1, 0, -1):
        push(h_front.at[front], h_front.at[front], H_FRONT, (leaf, flip(front, k)))
    drain(g_leaf.at[pl.ds(0, leaves - 1)], recv.at[G_LEAF])
    gram = jnp.sum(g_leaf[...], axis=0)[:, 0:basis]
    drain(h_front.at[pl.ds(0, fronts - 1)], recv.at[H_FRONT])
    h_leaf[leaf] = jnp.sum(h_front[...], axis=0)
    for k in range(leaves - 1, 0, -1):
        push(h_leaf.at[leaf], h_leaf.at[leaf], H_LEAF, (flip(leaf, k), front))
    drain(s_buf.at[pl.ds(0, fronts - 1)], recv.at[S_ALL])
    rows_cols = (((1,), (0,)), ((), ()))
    twice = 2.0 * (
        lax.broadcasted_iota(jnp.int32, gram.shape, 0)
        == lax.broadcasted_iota(jnp.int32, gram.shape, 1)
    ).astype(jnp.float32) - gram
    bsub_v[...] = exact(twice, bsub_v[...], rows_cols)
    bsep_v[...] = exact(twice, bsep_v[...], rows_cols)
    drain(h_leaf.at[pl.ds(0, leaves - 1)], recv.at[H_LEAF])

    once = jnp.sum(h_leaf[...], axis=0)[:, 0:basis]
    orth_sub[...] = sol_v[...] - exact(once, bsub_v[...], rows_cols)
    top_sol = jnp.concatenate([s_buf[k] for k in range(fronts)], axis=1)
    orth_sep[...] = top_sol - exact(once, bsep_v[...], rows_cols)
    coef[...] = once + (once - exact(once, gram, rows_cols))

    drain(a_pair, send.at[A_PAIR])
    drain(a_recv, send.at[A_SUM])
    drain(t_buf.at[pl.ds(0, fronts - 1)], send.at[A_ALL])
    drain(b_recv, send.at[B_SUM])
    drain(l_buf.at[pl.ds(0, leaves - 1)], send.at[B_ALL])
    drain(c_recv, send.at[C_SUM])
    drain(s_buf.at[pl.ds(0, fronts - 1)], send.at[S_ALL])
    drain(d_buf.at[0, pl.ds(0, half - 1)], send.at[D_ALL])
    drain(d_buf.at[0], send.at[D_PAIR])
    drain(g_front.at[pl.ds(0, fronts - 1)], send.at[G_FRONT])
    drain(g_leaf.at[pl.ds(0, leaves - 1)], send.at[G_LEAF])
    drain(h_front.at[pl.ds(0, fronts - 1)], send.at[H_FRONT])
    drain(h_leaf.at[pl.ds(0, leaves - 1)], send.at[H_LEAF])


def fused_shards(
    leaves,
    fronts,
    rhs_sub,
    rhs_sep,
    live_rows,
    lower_inv,
    upper_inv,
    couple_low,
    couple_up,
    sep_lower_inv,
    sep_upper_inv,
    basis_sub,
    basis_sep,
):
    vecs, basis = rhs_sub.shape[0], basis_sub.shape[0]
    half = leaves * fronts // 2
    width = rhs_sep.shape[1] // fronts
    size = lower_inv.shape[1]
    full = [
        rhs_sub, rhs_sep, lower_inv, upper_inv, couple_low, couple_up,
        sep_lower_inv, sep_upper_inv, basis_sub, basis_sep,
    ]
    lanes = -(-basis // 128) * 128
    narrow = (2 * vecs, width // 2)

    def wide(*shape):
        return pltpu.VMEM(shape, jnp.float32)

    def slim(slots):
        return pltpu.VMEM((slots,) + narrow, jnp.bfloat16)

    vmem = pl.BlockSpec(memory_space=pltpu.VMEM)
    anywhere = pl.BlockSpec(memory_space=pltpu.HBM)
    parts = pl.pallas_call(
        functools.partial(fused, leaves, fronts),
        out_shape=(
            jax.ShapeDtypeStruct(rhs_sub.shape, jnp.float32),
            jax.ShapeDtypeStruct(rhs_sep.shape, jnp.float32),
            jax.ShapeDtypeStruct((vecs, basis), jnp.float32),
        ),
        in_specs=[anywhere] * (len(full) + 1),
        out_specs=(vmem, vmem, vmem),
        scratch_shapes=[pltpu.VMEM(x.shape, x.dtype) for x in full]
        + [
            wide(vecs, size),
            wide(*rhs_sub.shape),
            wide(2, half, vecs, width),
            wide(half, vecs, width),
            slim(half),
            slim(half - 1),
            slim(fronts),
            wide(leaves, vecs, width),
            slim(leaves - 1),
            slim(leaves - 1),
            slim(leaves),
            wide(fronts, width, vecs),
            wide(fronts - 1, vecs, width),
            wide(fronts - 1, vecs, width),
            wide(fronts, vecs, width),
            pltpu.VMEM((2, half) + narrow, jnp.bfloat16),
            wide(fronts, basis, lanes),
            wide(leaves, basis, lanes),
            wide(fronts, vecs, lanes),
            wide(leaves, vecs, lanes),
            pltpu.SemaphoreType.DMA((12,)),
            pltpu.SemaphoreType.DMA((13,)),
            pltpu.SemaphoreType.DMA((13,)),
            pltpu.SemaphoreType.DMA((2,)),
            pltpu.SemaphoreType.DMA((fronts,)),
            pltpu.SemaphoreType.DMA((leaves,)),
            pltpu.SMEM(live_rows.shape, jnp.int32),
        ],
        compiler_params=pltpu.CompilerParams(
            collective_id=0, has_side_effects=True, vmem_limit_bytes=56 * 1024 * 1024
        ),
    )(live_rows, *full)
    orth_sub, orth_sep, coef = pl.pallas_call(
        hand_over,
        out_shape=tuple(jax.ShapeDtypeStruct(x.shape, x.dtype) for x in parts),
        in_specs=[anywhere] * 3,
        out_specs=(anywhere,) * 3,
        scratch_shapes=[pltpu.VMEM(x.shape, x.dtype) for x in parts]
        + [pltpu.SemaphoreType.DMA((3,))] * 2,
        compiler_params=pltpu.CompilerParams(vmem_limit_bytes=56 * 1024 * 1024),
    )(*parts)
    return orth_sub, orth_sep, coef.T


def apply_blocks(vectors, inverse):
    vec_count = vectors.shape[0]
    shaped = vectors.astype(jnp.bfloat16).reshape(vec_count, inverse.shape[0], inverse.shape[1])
    product = jnp.einsum("vkr,krc->vkc", shaped, inverse, preferred_element_type=jnp.float32)
    return product.reshape(vec_count, inverse.shape[0] * inverse.shape[2])


def shards(
    rhs_sub,
    rhs_sep,
    live_rows,
    lower_inv,
    upper_inv,
    couple_low,
    couple_up,
    sep_lower_inv,
    sep_upper_inv,
    basis_sub,
    basis_sep,
):
    vec_count, row_count = rhs_sub.shape
    border = couple_low.shape[0]
    high = lax.Precision.HIGHEST
    live_mask = lax.broadcasted_iota(jnp.int32, (1, row_count), 1) < live_rows[0]
    lower_sol = jnp.where(live_mask, apply_blocks(rhs_sub, lower_inv), 0.0)
    border_rows = lower_sol[:, :border].astype(jnp.bfloat16)
    columns = couple_low
    top_block = lax.psum_scatter(
        lax.dot_general(
            columns, border_rows, (((0,), (1,)), ((), ())), preferred_element_type=jnp.float32
        ),
        "leaf",
        scatter_dimension=0,
        tiled=True,
    )
    top_block = lax.psum(top_block, "front")
    top_rhs = rhs_sep - top_block.T
    lower_part = jnp.dot(
        top_rhs.astype(jnp.bfloat16), sep_lower_inv, preferred_element_type=jnp.float32
    )
    top_lower = lax.psum(lower_part, "leaf")
    upper_part = lax.dot_general(
        top_lower.astype(jnp.bfloat16),
        sep_upper_inv,
        (((1,), (1,)), ((), ())),
        preferred_element_type=jnp.float32,
    )
    top_sol = lax.psum(upper_part, "front")
    columns = couple_up
    correction = lax.dot_general(
        lax.all_gather(top_sol.astype(jnp.bfloat16), "leaf", axis=1, tiled=True),
        columns,
        (((1,), (1,)), ((), ())),
        preferred_element_type=jnp.float32,
    )
    updated = jnp.concatenate([lower_sol[:, :border] - correction, lower_sol[:, border:]], axis=1)
    upper_sol = jnp.where(live_mask, apply_blocks(updated, upper_inv), 0.0)
    coef_sum = jnp.zeros((basis_sub.shape[0], vec_count), jnp.float32)
    for sweep in range(2):
        local_sub = lax.dot_general(basis_sub, upper_sol, (((1,), (1,)), ((), ())), precision=high)
        local_sep = lax.dot_general(basis_sep, top_sol, (((1,), (1,)), ((), ())), precision=high)
        coef_pass = lax.psum(local_sub, ("leaf", "front")) + lax.psum(local_sep, "leaf")
        part_sub = upper_sol
        part_sep = top_sol
        part_sub = part_sub - lax.dot_general(
            coef_pass, basis_sub, (((0,), (0,)), ((), ())), precision=high
        )
        part_sep = part_sep - lax.dot_general(
            coef_pass, basis_sep, (((0,), (0,)), ((), ())), precision=high
        )
        upper_sol = part_sub
        top_sol = part_sep
        coef_sum = coef_sum + coef_pass
    return (upper_sol, top_sol, coef_sum)


def solution(mesh):
    leaves, fronts = mesh.shape["leaf"], mesh.shape["front"]

    def local(*arrays):
        piece = arrays[1].shape[1] // fronts
        paired = leaves > 2 and fronts > 2 and not (leaves & (leaves - 1) or fronts & (fronts - 1))
        if paired and piece % 256 == 0 and arrays[0].shape[0] == 8:
            return fused_shards(leaves, fronts, *arrays)
        return shards(*arrays)

    return jax.shard_map(
        local,
        mesh=mesh,
        in_specs=(
            P(None, ("leaf", "front")),
            P(None, "leaf"),
            P(("leaf", "front")),
            P(("leaf", "front"), None, None),
            P(("leaf", "front"), None, None),
            P(("leaf", "front"), None),
            P(("leaf", "front"), None),
            P("leaf", "front"),
            P("leaf", "front"),
            P(None, ("leaf", "front")),
            P(None, "leaf"),
        ),
        out_specs=(P(None, ("leaf", "front")), P(None, "leaf"), P()),
        check_vma=False,
    )
```
